32 devices in a mesh: depth: 4 (over y, x), row: 8 (over z, core).
Axes of the slice: x: 2, y: 2, z: 4, core: 2. Of those that a mesh axis runs over, the one named last changes fastest.
Arguments:
- index_volume: bfloat16 [4, 128, 2048], P('depth', 'row'), may hold values from -4 to 4
- angles: int32 [2], replicated, may hold values from 0 to 15
- offsets: int32 [4], P('depth'), may hold values from -4 to 4, as said below
- measured: bfloat16 [2, 128, 2048], P(None, 'row'), may hold values from 0 to 2
Outputs:
- gradient: float32 [4, 128, 2048], P('depth', 'row')
The draws below stay inside these ranges and needn't reach their ends.
Inputs may be any that keep to these rules, and one draw needn't show every extreme that they name: `offsets`: each of -4 and 4 is taken by at least one slice.
All inputs are finite; a program needn't handle non-finite values.
Results may differ from the reference program's by a relative error of at most 0.0003.
Values may be sent and summed in bfloat16 or wider, within the bound.
No kernel may reach another device: no remote copies, remote signals or barrier semaphores. Data moves between devices by JAX's collectives and lax.ppermute only.
A program may use at most 64 MiB of HBM per device.

```python
import math
import jax
import jax.numpy as jnp
from jax import lax

NX = 2048
ANG = 2
TILTS = 16
HALF = 10
SHIFT = 4
HALFCOL = 64
NY = 128
SLICES = 4


def draw_offsets(key, part):
    values = jax.random.randint(key, (SLICES,), -SHIFT, SHIFT + 1)
    ranking = jax.random.permutation(jax.random.fold_in(key, 7), SLICES)
    values = values.at[ranking[0]].set(SHIFT)
    values = values.at[ranking[1]].set(-SHIFT)
    return values.astype(jnp.int32)


def steps_of(own_key, dims, shards, low, top_value):
    def one(dim, blocks):
        steps = jax.random.uniform(jax.random.fold_in(jax.random.fold_in(own_key, 6), dim), (blocks,), jnp.float32, low / len(shards), top_value / len(shards))
        return jnp.repeat(jnp.exp(steps), dims[dim] // blocks).reshape((-1,) + (1,) * (len(dims) - dim - 1))

    level = one(*shards[0])
    for cut in shards[1:]:
        level = level * one(*cut)
    return level


def normal_values(rng, shape, width, limit, split=(), kind=jnp.bfloat16):
    array = jax.random.normal(rng, shape, jnp.float32) * width
    if len(split) > 0:
        array = steps_of(rng, shape, split, -0.22, 0.18) * array
    return jnp.clip(array, min=-limit, max=limit).astype(kind)


def setup_inputs(seed: int = 0) -> dict:
    streams_of = jax.random.split(jax.random.key(seed), 5)
    index_volume = normal_values(streams_of[0], (SLICES, NY, NX), 1.0, 4.0, ((0, 4), (1, 8)))
    angles = jax.random.randint(streams_of[1], (ANG,), 0, TILTS).astype(jnp.int32)
    offsets = draw_offsets(jax.random.fold_in(streams_of[4], 71), 0)
    measured = jnp.clip(2.0 * jax.random.uniform(streams_of[3], (ANG, NY, NX), jnp.float32) ** steps_of(streams_of[3], (ANG, NY, NX), ((1, 8),), -0.2, 0.2), 0.0, 2.0).astype(jnp.bfloat16)
    return dict(index_volume=index_volume, angles=angles, offsets=offsets, measured=measured)


PHASE_SCALE = 0.5
CHIRP_ROW = 1.3
CHIRP_COL = 1.7

def kernel_taps(radius, chirp_rate):
    distance = jnp.arange(-radius, radius + 1).astype(jnp.float32)
    phase_arg = chirp_rate / radius * distance * distance
    weight = 1.0 / math.sqrt(2 * radius + 1)
    return (jnp.cos(phase_arg) * weight, jnp.sin(phase_arg) * weight)

def plane_waves(angles, row_start, height, columns, total_rows):
    across = angles - TILTS // 2
    along = jnp.mod(3 * angles, TILTS) - TILTS // 2
    row_index = row_start + lax.broadcasted_iota(jnp.int32, (height, columns), 0)
    col_index = lax.broadcasted_iota(jnp.int32, (height, columns), 1)
    period = columns * total_rows
    cycles_int = jnp.mod(across[:, None, None] * col_index[None] * total_rows + along[:, None, None] * row_index[None] * columns, period).astype(jnp.int32)
    phase_arg = 2.0 * math.pi / period * cycles_int.astype(jnp.float32)
    return jnp.stack([jnp.cos(phase_arg), jnp.sin(phase_arg)], axis=1)

def banded(real_part, imag_part, taps, radius, offset, axis_no):
    length = real_part.shape[axis_no]
    padded_len = 1 << (length + 2 * radius).bit_length()
    spectrum = jnp.fft.fft(real_part + 1j * imag_part, n=padded_len, axis=axis_no)
    kernel = jnp.fft.fft(taps[0] + 1j * taps[1], n=padded_len)
    extent = [1] * real_part.ndim
    extent[axis_no] = padded_len
    full_conv = jnp.fft.ifft(spectrum * kernel.reshape(extent), axis=axis_no)
    window = lax.dynamic_slice_in_dim(full_conv, offset + radius, length, axis_no)
    return (jnp.real(window), jnp.imag(window))

def reference(index_volume, angles, offsets, measured):
    incident = plane_waves(angles, 0, NY, NX, NY)
    row_taps = kernel_taps(HALF, CHIRP_ROW)
    col_taps = kernel_taps(HALFCOL, CHIRP_COL)
    intensity = measured.astype(jnp.float32)

    def loss_value(volume):
        real_part = incident[:, 0]
        imag_part = incident[:, 1]
        for layer_no in range(SLICES):
            phase_arg = PHASE_SCALE * volume[layer_no]
            cosine = jnp.cos(phase_arg)
            sine = jnp.sin(phase_arg)
            real_part, imag_part = (cosine * real_part - sine * imag_part, cosine * imag_part + sine * real_part)
            real_part, imag_part = banded(real_part, imag_part, row_taps, HALF, offsets[layer_no], 1)
            real_part, imag_part = banded(real_part, imag_part, col_taps, HALFCOL, 0, 2)
        errors = real_part * real_part + imag_part * imag_part - intensity
        return 0.5 * jnp.sum(errors * errors)
    volume = index_volume.astype(jnp.float32)
    return jax.grad(loss_value)(volume)
```

```python
import functools
import math

import jax
import jax.numpy as jnp
import numpy as np
from jax import lax
from jax.experimental import pallas as pl
from jax.experimental.pallas import tpu as pltpu
from jax.sharding import PartitionSpec as P

TILTS = 16
HALF = 10
SHIFT = 4
HALFCOL = 64
COLBLK = 128


PHASE_SCALE = 0.5
CHIRP_ROW = 1.3
CHIRP_COL = 1.7


def padded_2(shard, sides, width):
    for axis, dim in sides:
        size, length = (lax.axis_size(axis), shard.shape[dim])
        up = [(i, (i + 1) % size) for i in range(size - 1)]
        down = [(j, i) for i, j in up]
        last = lax.slice_in_dim(shard, length - width, length, axis=dim)
        initial = lax.slice_in_dim(shard, 0, width, axis=dim)
        before = lax.ppermute(last, axis, up)
        after = lax.ppermute(initial, axis, down)
        shard = jnp.concatenate([before, shard, after], axis=dim)
    return shard


def from_behind(shard, axis, by):
    length = lax.axis_size(axis)
    pairs = [(i, i + by) for i in range(length) if 0 <= i + by < length]
    return lax.ppermute(shard, axis, pairs)


def kernel_values(distance, radius, chirp_rate):
    inside = jnp.abs(distance) <= radius
    phase_arg = chirp_rate / radius * distance * distance
    weight = 1.0 / math.sqrt(2 * radius + 1)
    real_part = jnp.where(inside, jnp.cos(phase_arg) * weight, 0.0)
    imag_part = jnp.where(inside, jnp.sin(phase_arg) * weight, 0.0)
    return (real_part, imag_part)


def row_band(offset, height, margin, conjugate):
    extent = (height, height + 2 * margin)
    target = lax.broadcasted_iota(jnp.int32, extent, 0)
    source = lax.broadcasted_iota(jnp.int32, extent, 1)
    offset_used = -offset if conjugate else offset
    distance = (source - target - margin - offset_used).astype(jnp.float32)
    real_part, imag_part = kernel_values(distance, HALF, CHIRP_ROW)
    return (real_part, -imag_part) if conjugate else (real_part, imag_part)


def column_band(conjugate, block_width):
    extent = (block_width + 2 * HALFCOL, block_width)
    source = lax.broadcasted_iota(jnp.int32, extent, 0)
    target = lax.broadcasted_iota(jnp.int32, extent, 1)
    distance = (source - target - HALFCOL).astype(jnp.float32)
    real_part, imag_part = kernel_values(distance, HALFCOL, CHIRP_COL)
    return (real_part, -imag_part) if conjugate else (real_part, imag_part)


def mix_rows(band, extended):

    def product(matrix, operand):
        return jnp.einsum("ij,mjc->mic", matrix, operand, precision=lax.Precision.HIGHEST)

    real_part = product(band[0], extended[:, 0]) - product(band[1], extended[:, 1])
    imag_part = product(band[0], extended[:, 1]) + product(band[1], extended[:, 0])
    return jnp.stack([real_part, imag_part], axis=1)


def block_product(window, band):

    def product(operand, matrix):
        return jnp.einsum("mrbj,ji->mrbi", operand, matrix, precision=lax.Precision.HIGHEST)

    real_part = product(window[:, 0], band[0]) - product(window[:, 1], band[1])
    imag_part = product(window[:, 1], band[0]) + product(window[:, 0], band[1])
    return jnp.stack([real_part, imag_part], axis=1)


def mix_columns(band, field):
    amount, _, height, columns = field.shape
    blocks = columns // COLBLK
    padded = jnp.pad(field, ((0, 0), (0, 0), (0, 0), (HALFCOL, COLBLK - HALFCOL)))
    middle = padded[..., :columns].reshape(amount, 2, height, blocks, COLBLK)
    beyond = padded[..., COLBLK : columns + COLBLK].reshape(amount, 2, height, blocks, COLBLK)
    window = jnp.concatenate([middle, beyond], axis=4)
    return block_product(window, band).reshape(amount, 2, height, columns)


def rotate(field, cosine, sine):
    real_part = cosine * field[:, 0] - sine * field[:, 1]
    imag_part = cosine * field[:, 1] + sine * field[:, 0]
    return jnp.stack([real_part, imag_part], axis=1)


def slab_forward(field, index_volume, offsets, active):
    margin = HALF + SHIFT
    height = field.shape[2]
    col_band = column_band(False, COLBLK)
    phase_arg = PHASE_SCALE * index_volume[0].astype(jnp.float32)
    transmitted = rotate(field, jnp.cos(phase_arg), jnp.sin(phase_arg))
    stored_fields = [transmitted]
    extended = padded_2(transmitted, (("row", 2),), margin)
    band = row_band(offsets[0], height, margin, False)

    def advance(operand, band=band):
        return mix_columns(col_band, mix_rows(band, operand))

    def remain(operand):
        return operand[:, :, margin : margin + height, :]

    field = lax.cond(active, advance, remain, extended)
    return (field, jnp.stack(stored_fields, axis=0))


def slab_adjoint(adjoint, stored, index_volume, offsets, active):
    margin = HALF + SHIFT
    height = adjoint.shape[2]
    col_band = column_band(True, COLBLK)
    layers = index_volume.shape[0]
    slab_grads = [None] * layers

    def column_step(operand):
        return mix_columns(col_band, operand)

    def unchanged(operand):
        return operand

    def remain(operand):
        return operand[:, :, margin : margin + height, :]

    for layer_no in reversed(range(layers)):
        returned = lax.cond(active, column_step, unchanged, adjoint)
        extended = padded_2(returned, (("row", 2),), margin)
        band = row_band(offsets[layer_no], height, margin, True)

        def row_step(operand, band=band):
            return mix_rows(band, operand)

        returned = lax.cond(active, row_step, remain, extended)
        transmitted = stored[layer_no]
        slab_grads[layer_no] = PHASE_SCALE * jnp.sum(
            transmitted[:, 0] * returned[:, 1] - transmitted[:, 1] * returned[:, 0], axis=0
        )
        phase_arg = PHASE_SCALE * index_volume[layer_no].astype(jnp.float32)
        adjoint = rotate(returned, jnp.cos(phase_arg), -jnp.sin(phase_arg))
    return (adjoint, jnp.stack(slab_grads, axis=0))


def plane_waves(angles, row_start, height, columns, total_rows, total_cols):
    across = angles - TILTS // 2
    along = jnp.mod(3 * angles, TILTS) - TILTS // 2
    row_index = row_start + lax.broadcasted_iota(jnp.int32, (height, columns), 0)
    col_index = lax.broadcasted_iota(jnp.int32, (height, columns), 1)
    period = total_cols * total_rows
    cycles_int = jnp.mod(
        across[:, None, None] * col_index[None] * total_rows
        + along[:, None, None] * row_index[None] * total_cols,
        period,
    )
    phase_arg = 2.0 * math.pi / period * cycles_int.astype(jnp.float32)
    return jnp.stack([jnp.cos(phase_arg), jnp.sin(phase_arg)], axis=1)


def body(index_volume, angles, offsets, measured):
    sections = lax.axis_size("depth")
    section_no = lax.axis_index("depth")
    number = angles.shape[0]
    layers = index_volume.shape[0]
    height = index_volume.shape[1]
    columns = index_volume.shape[2]
    row_start = lax.axis_index("row") * height
    total_rows = height * lax.axis_size("row")
    intensity = measured.astype(jnp.float32)
    grad_init = jnp.zeros((layers, height, columns), jnp.float32)
    incident = plane_waves(angles, row_start, height, columns, total_rows, columns)
    kept_init = jnp.zeros((layers,) + incident.shape, jnp.float32)

    def forward_compute(counter, received, stored, exit_field):
        angle_no = counter - section_no
        active = (angle_no >= 0) & (angle_no < number)
        chosen = jnp.clip(angle_no, 0, number - 1)
        entering = jnp.where(
            section_no == 0, lax.dynamic_slice_in_dim(incident, chosen, 1, 0), received
        )
        result, kept = slab_forward(entering, index_volume, offsets, active)
        placed_kept = lax.dynamic_update_slice_in_dim(stored, kept, chosen, 1)
        stored = jnp.where(active, placed_kept, stored)
        placed = lax.dynamic_update_slice_in_dim(exit_field, result, chosen, 0)
        exit_field = jnp.where(active, placed, exit_field)
        return (result, stored, exit_field)

    def forward_turn(counter, carried):
        result, stored, exit_field = forward_compute(counter, carried[0], carried[1], carried[2])
        return (from_behind(result, "depth", 1), stored, exit_field)

    zero_single = jnp.zeros((1,) + incident.shape[1:], jnp.float32)
    turns = sections + number - 1
    received, stored, exit_field = lax.fori_loop(
        0, turns - 1, forward_turn, (zero_single, kept_init, jnp.zeros_like(incident))
    )
    leftover, stored, exit_field = forward_compute(turns - 1, received, stored, exit_field)
    errors = exit_field[:, 0] * exit_field[:, 0] + exit_field[:, 1] * exit_field[:, 1] - intensity
    exit_adjoint = 2.0 * errors[:, None] * exit_field

    def backward_compute(counter, received, gradient):
        angle_no = counter - (sections - 1 - section_no)
        active = (angle_no >= 0) & (angle_no < number)
        chosen = jnp.clip(angle_no, 0, number - 1)
        entering = jnp.where(
            section_no == sections - 1,
            lax.dynamic_slice_in_dim(exit_adjoint, chosen, 1, 0),
            received,
        )
        result, slab_terms = slab_adjoint(
            entering, lax.dynamic_slice_in_dim(stored, chosen, 1, 1), index_volume, offsets, active
        )
        return (result, jnp.where(active, gradient + slab_terms, gradient))

    def backward_turn(counter, carried):
        result, gradient = backward_compute(counter, carried[0], carried[1])
        return (from_behind(result, "depth", -1), gradient)

    received, gradient = lax.fori_loop(0, turns - 1, backward_turn, (zero_single, grad_init))
    leftover, gradient = backward_compute(turns - 1, received, gradient)
    return gradient


def taps_of(radius, chirp_rate):
    distance = np.arange(-radius, radius + 1, dtype=np.float64)
    phase_arg = chirp_rate / radius * distance * distance
    weight = 1.0 / math.sqrt(2 * radius + 1)
    return (np.cos(phase_arg) * weight, np.sin(phase_arg) * weight)


def split_constant(matrix):
    high = matrix.astype(jnp.bfloat16)
    low = (matrix - high.astype(np.float64)).astype(jnp.bfloat16)
    return (high, low)


def column_weights(conjugate):
    taps = taps_of(HALFCOL, CHIRP_COL)
    source = np.arange(COLBLK + 2 * HALFCOL)[:, None]
    target = np.arange(COLBLK)[None, :]
    place = source - target
    inside = (place >= 0) & (place <= 2 * HALFCOL)
    real_part, imag_part = [np.where(inside, t[np.clip(place, 0, 2 * HALFCOL)], 0.0) for t in taps]
    if conjugate:
        imag_part = -imag_part
    from_real = split_constant(np.concatenate([real_part, imag_part], axis=1))
    from_imag = split_constant(np.concatenate([-imag_part, real_part], axis=1))
    return np.stack(from_real + from_imag)


def series(kind):
    nodes = np.cos((np.arange(40) + 0.5) * np.pi / 40) * 8.0 + 8.0
    x = np.sqrt(nodes)
    values = np.cos(PHASE_SCALE * x) if kind == "cos" else np.sin(PHASE_SCALE * x) / x
    fitted = np.polynomial.chebyshev.Chebyshev.fit(nodes, values, 6, domain=[0.0, 16.0])
    return [float(v) for v in fitted.convert(kind=np.polynomial.Polynomial).coef]


COS_SERIES = series("cos")
SIN_SERIES = series("sin")


def evaluate(coefficients, x):
    total = x * coefficients[-1] + coefficients[-2]
    for value in coefficients[-3::-1]:
        total = total * x + value
    return total


def split(x):
    high = x.astype(jnp.bfloat16)
    return (high, (x - high.astype(jnp.float32)).astype(jnp.bfloat16))


def dot(a, b):
    return jnp.dot(a, b, preferred_element_type=jnp.float32)


def row_factor(rows_of, rows_across, offset):
    n = rows_of.shape[0]
    distance = jnp.abs(rows_across - rows_of - offset)
    cosines, sines = taps_of(HALF, CHIRP_ROW)
    real_part = jnp.zeros((n, n), jnp.float32)
    imag_part = jnp.zeros((n, n), jnp.float32)
    for k in range(HALF + 1):
        hit = distance == k
        real_part = jnp.where(hit, float(cosines[HALF + k]), real_part)
        imag_part = jnp.where(hit, float(sines[HALF + k]), imag_part)
    return (real_part, imag_part)


def complex_form(real_part, imag_part):
    upper = jnp.concatenate([real_part, -imag_part], axis=1)
    lower = jnp.concatenate([imag_part, real_part], axis=1)
    return jnp.concatenate([upper, lower], axis=0)


def sweep(sizes, where, own, other, measured, forward_cols, adjoint_cols, out, cosine, sine, field, windows, kept):
    slices, planes, height, blocks, columns = sizes
    half = planes * height
    rows = 2 * half
    across, along, block, plane, core, place = [where[i] for i in range(6)]

    def row_numbers(axis):
        i = lax.broadcasted_iota(jnp.int32, (rows, rows), axis)
        side = i // half
        step = (i - side * half) // height
        return 2 * height * (plane ^ step) + height * (core ^ side) + i % height

    rows_of, rows_across = row_numbers(0), row_numbers(1)
    factors = [row_factor(rows_of, rows_across, where[6 + s]) for s in range(slices)]
    width = blocks * COLBLK
    first = block * COLBLK - 2 * slices * HALFCOL
    lane = first + lax.broadcasted_iota(jnp.int32, (1, width), 1)
    inside = (lane >= 0) & (lane < columns)
    for s in range(slices):
        slot = place ^ s
        for part, source in enumerate((own, other)):
            x = source[slot].astype(jnp.float32)
            square = x * x
            c = jnp.where(inside, evaluate(COS_SERIES, square), 0.0)
            d = jnp.where(inside, evaluate(SIN_SERIES, square) * x, 0.0)
            skip = s * HALFCOL
            used = width - 2 * skip
            cosine[s, part * half : (part + 1) * half, :used] = c[:, skip : skip + used]
            sine[s, part * half : (part + 1) * half, :used] = d[:, skip : skip + used]

    turn = 2.0 * math.pi / columns
    col_phase = turn * (lax.rem(across * lane, columns)).astype(jnp.float32)
    row_phase = 2.0 * math.pi / rows * (lax.rem(along * row_numbers(0)[:, :1], rows)).astype(jnp.float32)
    row_cos, row_sin = jnp.cos(row_phase), jnp.sin(row_phase)
    col_cos, col_sin = jnp.cos(col_phase), jnp.sin(col_phase)

    def to_windows(j, count, high, low):
        for part, (x, y) in enumerate(((high[0], low[0]), (high[1], low[1]))):
            if j < count:
                windows[2 * part, j * rows : (j + 1) * rows, :COLBLK] = x
                windows[2 * part + 1, j * rows : (j + 1) * rows, :COLBLK] = y
            if j > 0:
                windows[2 * part, (j - 1) * rows : j * rows, COLBLK:] = x
                windows[2 * part + 1, (j - 1) * rows : j * rows, COLBLK:] = y

    def mix_cols(count, weights):
        n = count * rows
        total = dot(windows[0, :n], weights[0]) + dot(windows[2, :n], weights[2])
        total += dot(windows[1, :n], weights[0]) + dot(windows[3, :n], weights[2])
        total += dot(windows[0, :n], weights[1]) + dot(windows[2, :n], weights[3])
        field[:n] = total

    def mix_row_block(factor_high, factor_low, x):
        high, low = split(x)
        return dot(factor_high, high) + (dot(factor_high, low) + dot(factor_low, high))

    for s in range(slices):
        high, low = split(complex_form(*factors[s]))
        n = blocks - s
        for j in range(n):
            cols = slice(j * COLBLK, (j + 1) * COLBLK)
            c, d = cosine[s, :, cols], sine[s, :, cols]
            if s == 0:
                cc, cs = col_cos[:, cols], col_sin[:, cols]
                a = row_cos * cc - row_sin * cs
                b = row_cos * cs + row_sin * cc
            else:
                a = field[j * rows : (j + 1) * rows, :COLBLK]
                b = field[j * rows : (j + 1) * rows, COLBLK:]
            y = jnp.concatenate([c * a - d * b, c * b + d * a], axis=0)
            start = 2 * slices * HALFCOL - s * HALFCOL
            begin = j * COLBLK
            if begin < start + COLBLK and begin + COLBLK > start:
                lo, hi = max(start, begin), min(start + COLBLK, begin + COLBLK)
                kept[s, :, lo - start : hi - start] = y[:, lo - begin : hi - begin]
            v = mix_row_block(high, low, y)
            v_high, v_low = split(v)
            to_windows(j, n - 1, (v_high[:rows], v_high[rows:]), (v_low[:rows], v_low[rows:]))
        mix_cols(n - 1, forward_cols)

    n = blocks - slices
    for j in range(n):
        a = field[j * rows : (j + 1) * rows, :COLBLK]
        b = field[j * rows : (j + 1) * rows, COLBLK:]
        seen = jnp.concatenate(
            [measured[k, side, :, j * COLBLK : (j + 1) * COLBLK] for side in range(2) for k in range(planes)], axis=0
        ).astype(jnp.float32)
        begin = slices * HALFCOL + j * COLBLK
        error = 2.0 * (a * a + b * b - seen)
        error = jnp.where(inside[:, begin : begin + COLBLK], error, 0.0)
        a_high, a_low = split(error * a)
        b_high, b_low = split(error * b)
        to_windows(j, n - 1, (a_high, b_high), (a_low, b_low))

    for s in reversed(range(slices)):
        n -= 1
        mix_cols(n, adjoint_cols)
        real_part, imag_part = factors[s]
        high, low = split(complex_form(real_part.T, -imag_part.T))
        for j in range(n):
            a = field[j * rows : (j + 1) * rows, :COLBLK]
            b = field[j * rows : (j + 1) * rows, COLBLK:]
            v = mix_row_block(high, low, jnp.concatenate([a, b], axis=0))
            a, b = v[:rows], v[rows:]
            begin = s * HALFCOL - j * COLBLK
            if -COLBLK < begin < COLBLK:
                lo, hi = max(begin, 0), min(begin + COLBLK, COLBLK)
                y = kept[s, :, lo - begin : hi - begin]
                part = PHASE_SCALE * (y[:rows] * b[:, lo:hi] - y[rows:] * a[:, lo:hi])
                out[place ^ s, :, lo - begin : hi - begin] = part
            if s > 0:
                shift = (2 * slices * HALFCOL - s * HALFCOL) - s * HALFCOL + j * COLBLK
                c = cosine[s, :, shift : shift + COLBLK]
                d = sine[s, :, shift : shift + COLBLK]
                a_high, a_low = split(c * a + d * b)
                b_high, b_low = split(c * b - d * a)
                to_windows(j, n - 1, (a_high, b_high), (a_low, b_low))


def swap(x, axis, step):
    size = lax.axis_size(axis)
    return lax.ppermute(x, axis, [(i, i ^ step) for i in range(size)])


def window_body(index_volume, angles, offsets, measured):
    slices = lax.axis_size("depth")
    planes = lax.axis_size("row") // 2
    place = lax.axis_index("depth")
    core = lax.axis_index("row") % 2
    plane = lax.axis_index("row") // 2
    height, columns = index_volume.shape[1:]
    rows = 2 * planes * height
    span = slices * COLBLK
    cone = 2 * slices * HALFCOL
    blocks = 1 + 2 * cone // COLBLK

    padded = jnp.pad(index_volume[0], ((0, 0), (cone, cone)))
    pieces = [lax.dynamic_slice_in_dim(padded, span * (plane ^ k), span + 2 * cone, 1) for k in range(planes)]
    pieces = [pieces[0]] + [swap(pieces[k], "row", 2 * k) for k in range(1, planes)]
    own_slice = jnp.stack(pieces)
    parts = [lax.dynamic_slice_in_dim(own_slice, COLBLK * (place ^ j), blocks * COLBLK, 2) for j in range(slices)]
    parts = [parts[0]] + [swap(parts[j], "depth", j) for j in range(1, slices)]
    own = jnp.stack(parts).reshape(slices, planes * height, blocks * COLBLK)
    other = swap(own, "row", 1)

    all_offsets = jnp.stack([offsets[0]] + [swap(offsets, "depth", j)[0] for j in range(1, slices)])
    all_offsets = jnp.stack([all_offsets[place ^ s] for s in range(slices)])

    mine = lax.dynamic_index_in_dim(measured, core, 0, False)
    theirs = swap(lax.dynamic_index_in_dim(measured, 1 - core, 0, False), "row", 1)
    both = jnp.pad(jnp.stack([mine, theirs]), ((0, 0), (0, 0), (cone // 2, cone // 2)))
    seen = [lax.dynamic_slice_in_dim(both, span * (plane ^ k), span + cone, 2) for k in range(planes)]
    seen = jnp.stack([seen[0]] + [swap(seen[k], "row", 2 * k) for k in range(1, planes)])
    seen = lax.dynamic_slice_in_dim(seen, COLBLK * place, COLBLK + cone, 3)

    angle = angles[core]
    across = angle - TILTS // 2
    along = jnp.mod(3 * angle, TILTS) - TILTS // 2
    where = jnp.concatenate(
        [jnp.stack([across, along, plane * slices + place, plane, core, place]), all_offsets]
    ).astype(jnp.int32)

    width = blocks * COLBLK
    sizes = (slices, planes, height, blocks, columns)
    result = pl.pallas_call(
        functools.partial(sweep, sizes),
        out_shape=jax.ShapeDtypeStruct((slices, rows, COLBLK), jnp.float32),
        in_specs=[pl.BlockSpec(memory_space=pltpu.SMEM)] + [pl.BlockSpec(memory_space=pltpu.VMEM)] * 5,
        out_specs=pl.BlockSpec(memory_space=pltpu.VMEM),
        scratch_shapes=[
            pltpu.VMEM((slices, rows, width), jnp.float32),
            pltpu.VMEM((slices, rows, width), jnp.float32),
            pltpu.VMEM(((blocks - 1) * rows, 2 * COLBLK), jnp.float32),
            pltpu.VMEM((4, (blocks - 1) * rows, 2 * COLBLK), jnp.bfloat16),
            pltpu.VMEM((slices, 2 * rows, COLBLK), jnp.float32),
        ],
        compiler_params=pltpu.CompilerParams(vmem_limit_bytes=48 * 1024 * 1024),
    )(where, own, other, seen, jnp.asarray(column_weights(False)), jnp.asarray(column_weights(True)))

    half = planes * height
    summed = result[:, :half] + swap(result[:, half:], "row", 1)
    parts = jnp.stack([summed[0]] + [swap(summed[j], "depth", j) for j in range(1, slices)])
    parts = parts.reshape(slices, planes, height, COLBLK)
    parts = jnp.stack([parts[place ^ j] for j in range(slices)])
    parts = parts.transpose(1, 2, 0, 3).reshape(planes, height, span)
    parts = jnp.stack([parts[0]] + [swap(parts[k], "row", 2 * k) for k in range(1, planes)])
    parts = jnp.stack([parts[plane ^ k] for k in range(planes)])
    return parts.transpose(1, 0, 2).reshape(1, height, columns)


def suits(mesh, index_volume, measured):
    depth, row = mesh.shape["depth"], mesh.shape["row"]
    slices, rows, columns = index_volume.shape
    return (
        slices == depth
        and depth & (depth - 1) == 0
        and row & (row - 1) == 0
        and row > 1
        and measured.shape[0] == 2
        and rows == COLBLK
        and rows // row % 16 == 0
        and columns == COLBLK * depth * (row // 2)
    )


def solution(mesh):
    in_specs = (P("depth", "row", None), P(), P("depth"), P(None, "row", None))
    out_specs = P("depth", "row", None)

    def run(index_volume, angles, offsets, measured):
        chosen = window_body if suits(mesh, index_volume, measured) else body
        mapped = jax.shard_map(chosen, mesh=mesh, in_specs=in_specs, out_specs=out_specs, check_vma=False)
        return mapped(index_volume, angles, offsets, measured)

    return run
```

```python
import functools
import math

import jax
import jax.numpy as jnp
import numpy as np
from jax import lax
from jax.experimental import pallas as pl
from jax.experimental.pallas import tpu as pltpu
from jax.sharding import PartitionSpec as P

TILTS = 16
HALF = 10
SHIFT = 4
HALFCOL = 64
COLBLK = 128


PHASE_SCALE = 0.5
CHIRP_ROW = 1.3
CHIRP_COL = 1.7


def padded_2(shard, sides, width):
    for axis, dim in sides:
        size, length = (lax.axis_size(axis), shard.shape[dim])
        up = [(i, (i + 1) % size) for i in range(size - 1)]
        down = [(j, i) for i, j in up]
        last = lax.slice_in_dim(shard, length - width, length, axis=dim)
        initial = lax.slice_in_dim(shard, 0, width, axis=dim)
        before = lax.ppermute(last, axis, up)
        after = lax.ppermute(initial, axis, down)
        shard = jnp.concatenate([before, shard, after], axis=dim)
    return shard


def from_behind(shard, axis, by):
    length = lax.axis_size(axis)
    pairs = [(i, i + by) for i in range(length) if 0 <= i + by < length]
    return lax.ppermute(shard, axis, pairs)


def kernel_values(distance, radius, chirp_rate):
    inside = jnp.abs(distance) <= radius
    phase_arg = chirp_rate / radius * distance * distance
    weight = 1.0 / math.sqrt(2 * radius + 1)
    real_part = jnp.where(inside, jnp.cos(phase_arg) * weight, 0.0)
    imag_part = jnp.where(inside, jnp.sin(phase_arg) * weight, 0.0)
    return (real_part, imag_part)


def row_band(offset, height, margin, conjugate):
    extent = (height, height + 2 * margin)
    target = lax.broadcasted_iota(jnp.int32, extent, 0)
    source = lax.broadcasted_iota(jnp.int32, extent, 1)
    offset_used = -offset if conjugate else offset
    distance = (source - target - margin - offset_used).astype(jnp.float32)
    real_part, imag_part = kernel_values(distance, HALF, CHIRP_ROW)
    return (real_part, -imag_part) if conjugate else (real_part, imag_part)


def column_band(conjugate, block_width):
    extent = (block_width + 2 * HALFCOL, block_width)
    source = lax.broadcasted_iota(jnp.int32, extent, 0)
    target = lax.broadcasted_iota(jnp.int32, extent, 1)
    distance = (source - target - HALFCOL).astype(jnp.float32)
    real_part, imag_part = kernel_values(distance, HALFCOL, CHIRP_COL)
    return (real_part, -imag_part) if conjugate else (real_part, imag_part)


def mix_rows(band, extended):

    def product(matrix, operand):
        return jnp.einsum("ij,mjc->mic", matrix, operand, precision=lax.Precision.HIGHEST)

    real_part = product(band[0], extended[:, 0]) - product(band[1], extended[:, 1])
    imag_part = product(band[0], extended[:, 1]) + product(band[1], extended[:, 0])
    return jnp.stack([real_part, imag_part], axis=1)


def block_product(window, band):

    def product(operand, matrix):
        return jnp.einsum("mrbj,ji->mrbi", operand, matrix, precision=lax.Precision.HIGHEST)

    real_part = product(window[:, 0], band[0]) - product(window[:, 1], band[1])
    imag_part = product(window[:, 1], band[0]) + product(window[:, 0], band[1])
    return jnp.stack([real_part, imag_part], axis=1)


def mix_columns(band, field):
    amount, _, height, columns = field.shape
    blocks = columns // COLBLK
    padded = jnp.pad(field, ((0, 0), (0, 0), (0, 0), (HALFCOL, COLBLK - HALFCOL)))
    middle = padded[..., :columns].reshape(amount, 2, height, blocks, COLBLK)
    beyond = padded[..., COLBLK : columns + COLBLK].reshape(amount, 2, height, blocks, COLBLK)
    window = jnp.concatenate([middle, beyond], axis=4)
    return block_product(window, band).reshape(amount, 2, height, columns)


def rotate(field, cosine, sine):
    real_part = cosine * field[:, 0] - sine * field[:, 1]
    imag_part = cosine * field[:, 1] + sine * field[:, 0]
    return jnp.stack([real_part, imag_part], axis=1)


def slab_forward(field, index_volume, offsets, active):
    margin = HALF + SHIFT
    height = field.shape[2]
    col_band = column_band(False, COLBLK)
    phase_arg = PHASE_SCALE * index_volume[0].astype(jnp.float32)
    transmitted = rotate(field, jnp.cos(phase_arg), jnp.sin(phase_arg))
    stored_fields = [transmitted]
    extended = padded_2(transmitted, (("row", 2),), margin)
    band = row_band(offsets[0], height, margin, False)

    def advance(operand, band=band):
        return mix_columns(col_band, mix_rows(band, operand))

    def remain(operand):
        return operand[:, :, margin : margin + height, :]

    field = lax.cond(active, advance, remain, extended)
    return (field, jnp.stack(stored_fields, axis=0))


def slab_adjoint(adjoint, stored, index_volume, offsets, active):
    margin = HALF + SHIFT
    height = adjoint.shape[2]
    col_band = column_band(True, COLBLK)
    layers = index_volume.shape[0]
    slab_grads = [None] * layers

    def column_step(operand):
        return mix_columns(col_band, operand)

    def unchanged(operand):
        return operand

    def remain(operand):
        return operand[:, :, margin : margin + height, :]

    for layer_no in reversed(range(layers)):
        returned = lax.cond(active, column_step, unchanged, adjoint)
        extended = padded_2(returned, (("row", 2),), margin)
        band = row_band(offsets[layer_no], height, margin, True)

        def row_step(operand, band=band):
            return mix_rows(band, operand)

        returned = lax.cond(active, row_step, remain, extended)
        transmitted = stored[layer_no]
        slab_grads[layer_no] = PHASE_SCALE * jnp.sum(
            transmitted[:, 0] * returned[:, 1] - transmitted[:, 1] * returned[:, 0], axis=0
        )
        phase_arg = PHASE_SCALE * index_volume[layer_no].astype(jnp.float32)
        adjoint = rotate(returned, jnp.cos(phase_arg), -jnp.sin(phase_arg))
    return (adjoint, jnp.stack(slab_grads, axis=0))


def plane_waves(angles, row_start, height, columns, total_rows, total_cols):
    across = angles - TILTS // 2
    along = jnp.mod(3 * angles, TILTS) - TILTS // 2
    row_index = row_start + lax.broadcasted_iota(jnp.int32, (height, columns), 0)
    col_index = lax.broadcasted_iota(jnp.int32, (height, columns), 1)
    period = total_cols * total_rows
    cycles_int = jnp.mod(
        across[:, None, None] * col_index[None] * total_rows
        + along[:, None, None] * row_index[None] * total_cols,
        period,
    )
    phase_arg = 2.0 * math.pi / period * cycles_int.astype(jnp.float32)
    return jnp.stack([jnp.cos(phase_arg), jnp.sin(phase_arg)], axis=1)


def body(index_volume, angles, offsets, measured):
    sections = lax.axis_size("depth")
    section_no = lax.axis_index("depth")
    number = angles.shape[0]
    layers = index_volume.shape[0]
    height = index_volume.shape[1]
    columns = index_volume.shape[2]
    row_start = lax.axis_index("row") * height
    total_rows = height * lax.axis_size("row")
    intensity = measured.astype(jnp.float32)
    grad_init = jnp.zeros((layers, height, columns), jnp.float32)
    incident = plane_waves(angles, row_start, height, columns, total_rows, columns)
    kept_init = jnp.zeros((layers,) + incident.shape, jnp.float32)

    def forward_compute(counter, received, stored, exit_field):
        angle_no = counter - section_no
        active = (angle_no >= 0) & (angle_no < number)
        chosen = jnp.clip(angle_no, 0, number - 1)
        entering = jnp.where(
            section_no == 0, lax.dynamic_slice_in_dim(incident, chosen, 1, 0), received
        )
        result, kept = slab_forward(entering, index_volume, offsets, active)
        placed_kept = lax.dynamic_update_slice_in_dim(stored, kept, chosen, 1)
        stored = jnp.where(active, placed_kept, stored)
        placed = lax.dynamic_update_slice_in_dim(exit_field, result, chosen, 0)
        exit_field = jnp.where(active, placed, exit_field)
        return (result, stored, exit_field)

    def forward_turn(counter, carried):
        result, stored, exit_field = forward_compute(counter, carried[0], carried[1], carried[2])
        return (from_behind(result, "depth", 1), stored, exit_field)

    zero_single = jnp.zeros((1,) + incident.shape[1:], jnp.float32)
    turns = sections + number - 1
    received, stored, exit_field = lax.fori_loop(
        0, turns - 1, forward_turn, (zero_single, kept_init, jnp.zeros_like(incident))
    )
    leftover, stored, exit_field = forward_compute(turns - 1, received, stored, exit_field)
    errors = exit_field[:, 0] * exit_field[:, 0] + exit_field[:, 1] * exit_field[:, 1] - intensity
    exit_adjoint = 2.0 * errors[:, None] * exit_field

    def backward_compute(counter, received, gradient):
        angle_no = counter - (sections - 1 - section_no)
        active = (angle_no >= 0) & (angle_no < number)
        chosen = jnp.clip(angle_no, 0, number - 1)
        entering = jnp.where(
            section_no == sections - 1,
            lax.dynamic_slice_in_dim(exit_adjoint, chosen, 1, 0),
            received,
        )
        result, slab_terms = slab_adjoint(
            entering, lax.dynamic_slice_in_dim(stored, chosen, 1, 1), index_volume, offsets, active
        )
        return (result, jnp.where(active, gradient + slab_terms, gradient))

    def backward_turn(counter, carried):
        result, gradient = backward_compute(counter, carried[0], carried[1])
        return (from_behind(result, "depth", -1), gradient)

    received, gradient = lax.fori_loop(0, turns - 1, backward_turn, (zero_single, grad_init))
    leftover, gradient = backward_compute(turns - 1, received, gradient)
    return gradient


def taps_of(radius, chirp_rate):
    distance = np.arange(-radius, radius + 1, dtype=np.float64)
    phase_arg = chirp_rate / radius * distance * distance
    weight = 1.0 / math.sqrt(2 * radius + 1)
    return (np.cos(phase_arg) * weight, np.sin(phase_arg) * weight)


def split_constant(matrix):
    high = matrix.astype(jnp.bfloat16)
    low = (matrix - high.astype(np.float64)).astype(jnp.bfloat16)
    return (high, low)


def column_weights(conjugate):
    taps = taps_of(HALFCOL, CHIRP_COL)
    source = np.arange(COLBLK + 2 * HALFCOL)[:, None]
    target = np.arange(COLBLK)[None, :]
    place = source - target
    inside = (place >= 0) & (place <= 2 * HALFCOL)
    real_part, imag_part = [np.where(inside, t[np.clip(place, 0, 2 * HALFCOL)], 0.0) for t in taps]
    if conjugate:
        imag_part = -imag_part
    from_real = np.concatenate([real_part, imag_part], axis=1)
    from_imag = np.concatenate([-imag_part, real_part], axis=1)
    high, low = split_constant(np.concatenate([from_real, from_imag], axis=0))
    return np.concatenate([high, high, low], axis=0)


def series(kind):
    nodes = np.cos((np.arange(40) + 0.5) * np.pi / 40) * 8.0 + 8.0
    x = np.sqrt(nodes)
    values = np.cos(PHASE_SCALE * x) if kind == "cos" else np.sin(PHASE_SCALE * x) / x
    fitted = np.polynomial.chebyshev.Chebyshev.fit(nodes, values, 6, domain=[0.0, 16.0])
    return [float(v) for v in fitted.convert(kind=np.polynomial.Polynomial).coef]


COS_SERIES = series("cos")
SIN_SERIES = series("sin")


def evaluate(coefficients, x):
    total = x * coefficients[-1] + coefficients[-2]
    for value in coefficients[-3::-1]:
        total = total * x + value
    return total


def split(x):
    high = x.astype(jnp.bfloat16)
    return (high, (x - high.astype(jnp.float32)).astype(jnp.bfloat16))


def dot(a, b):
    return jnp.dot(a, b, preferred_element_type=jnp.float32)


def row_factor(rows_of, rows_across, offset):
    n = rows_of.shape[0]
    distance = jnp.abs(rows_across - rows_of - offset)
    cosines, sines = taps_of(HALF, CHIRP_ROW)
    real_part = jnp.zeros((n, n), jnp.float32)
    imag_part = jnp.zeros((n, n), jnp.float32)
    for k in range(HALF + 1):
        hit = distance == k
        real_part = jnp.where(hit, float(cosines[HALF + k]), real_part)
        imag_part = jnp.where(hit, float(sines[HALF + k]), imag_part)
    return (real_part, imag_part)


def complex_form(real_part, imag_part):
    upper = jnp.concatenate([real_part, -imag_part], axis=1)
    lower = jnp.concatenate([imag_part, real_part], axis=1)
    return jnp.concatenate([upper, lower], axis=0)


def sweep(sizes, angles, tiles, own, other, measured, forward_cols, adjoint_cols, mine, theirs, cosine, sine, field, kept):
    slices, planes, height, blocks, columns = sizes
    half = planes * height
    rows = 2 * half
    place = lax.axis_index("depth")
    core = lax.axis_index("row") % 2
    plane = lax.axis_index("row") // 2
    block = plane * slices + place
    angle = angles[core]
    across = angle - TILTS // 2
    along = lax.rem(3 * angle, TILTS) - TILTS // 2

    def row_numbers(axis):
        i = lax.broadcasted_iota(jnp.int32, (rows, rows), axis)
        side = i // half
        step = (i - side * half) // height
        return 2 * height * (plane ^ step) + height * (core ^ side) + i % height

    rows_of, rows_across = row_numbers(0), row_numbers(1)
    walk_off = [tiles[place ^ s, :1].astype(jnp.int32) for s in range(slices)]
    factors = [row_factor(rows_of, rows_across, offset) for offset in walk_off]
    width = blocks * COLBLK
    first = block * COLBLK - 2 * slices * HALFCOL
    lane = first + lax.broadcasted_iota(jnp.int32, (1, width), 1)
    inside = (lane >= 0) & (lane < columns)

    turn = 2.0 * math.pi / columns
    col_phase = turn * (lax.rem(across * lane, columns)).astype(jnp.float32)
    row_phase = 2.0 * math.pi / rows * (lax.rem(along * row_numbers(0)[:, :1], rows)).astype(jnp.float32)
    row_cos, row_sin = jnp.cos(row_phase), jnp.sin(row_phase)
    col_cos, col_sin = jnp.cos(col_phase), jnp.sin(col_phase)

    def read(level, j):
        return (field[level, j, :, :COLBLK], field[level, j, :, COLBLK:])

    def operand(a, b):
        a_high, a_low = split(a)
        b_high, b_low = split(b)
        return (a_high, b_high, a_low, b_low)

    def mix_cols(level, j, left, right, weights):
        wide = jnp.concatenate([part for pair in zip(left, right) for part in pair], axis=1)
        total = dot(wide, weights[: 8 * COLBLK]) + dot(wide[:, : 4 * COLBLK], weights[8 * COLBLK :])
        field[level, j] = total

    def mix_rows(factor, blocks_in):
        y = jnp.concatenate([jnp.concatenate([a, b], axis=0) for a, b in blocks_in], axis=1)
        y_high, y_low = split(y)
        v = dot(factor[0], y_high) + (dot(factor[0], y_low) + dot(factor[1], y_high))
        cut = [slice(i * COLBLK, (i + 1) * COLBLK) for i in range(len(blocks_in))]
        return [(v[:rows, c], v[rows:, c]) for c in cut]

    def pairs(n):
        return [range(j, min(j + 2, n)) for j in range(0, n, 2)]

    def forward(s):
        factor = split(complex_form(*factors[s]))
        slot = place ^ s
        last = None
        for group in pairs(blocks - s):
            turned = []
            for j in group:
                begin = s * HALFCOL + j * COLBLK
                x = jnp.concatenate([r[slot, :, begin : begin + COLBLK] for r in (own, other)], axis=0)
                x = x.astype(jnp.float32)
                square = x * x
                seen = inside[:, begin : begin + COLBLK]
                c = jnp.where(seen, evaluate(COS_SERIES, square), 0.0)
                d = jnp.where(seen, evaluate(SIN_SERIES, square) * x, 0.0)
                if s > 0:
                    cosine[s, :, j * COLBLK : (j + 1) * COLBLK] = c
                    sine[s, :, j * COLBLK : (j + 1) * COLBLK] = d
                if s == 0:
                    cc, cs = col_cos[:, begin : begin + COLBLK], col_sin[:, begin : begin + COLBLK]
                    a = row_cos * cc - row_sin * cs
                    b = row_cos * cs + row_sin * cc
                else:
                    a, b = read(s - 1, j)
                a, b = c * a - d * b, c * b + d * a
                start = (2 * slices - s) * HALFCOL - j * COLBLK
                lo, hi = max(start, 0), min(start + COLBLK, COLBLK)
                if lo < hi:
                    kept[s, :rows, lo - start : hi - start] = a[:, lo:hi]
                    kept[s, rows:, lo - start : hi - start] = b[:, lo:hi]
                turned.append((a, b))
            for j, v in zip(group, mix_rows(factor, turned)):
                parts = operand(*v)
                if j > 0:
                    mix_cols(s, j - 1, last, parts, forward_cols)
                last = parts
            yield

    def residual():
        last = None
        for group in pairs(blocks - slices):
            for j in group:
                a, b = read(slices - 1, j)
                cols = slice(j * COLBLK, (j + 1) * COLBLK)
                seen = [measured[k, side, :, cols] for side in range(2) for k in range(planes)]
                seen = jnp.concatenate(seen, axis=0).astype(jnp.float32)
                begin = slices * HALFCOL + j * COLBLK
                error = 2.0 * (a * a + b * b - seen)
                error = jnp.where(inside[:, begin : begin + COLBLK], error, 0.0)
                parts = operand(error * a, error * b)
                if j > 0:
                    mix_cols(slices, j - 1, last, parts, adjoint_cols)
                last = parts
            yield

    def backward(s):
        real_part, imag_part = factors[s]
        factor = split(complex_form(real_part.T, -imag_part.T))
        level = 2 * slices - 1 - s
        last = None
        for group in pairs(s + 1):
            for j, (a, b) in zip(group, mix_rows(factor, [read(level, j) for j in group])):
                start = s * HALFCOL - j * COLBLK
                lo, hi = max(start, 0), min(start + COLBLK, COLBLK)
                if lo < hi:
                    y = kept[s, :, lo - start : hi - start]
                    part = PHASE_SCALE * (y[:rows] * b[:, lo:hi] - y[rows:] * a[:, lo:hi])
                    mine[place ^ s, :, lo - start : hi - start] = part[:half]
                    theirs[place ^ s, :, lo - start : hi - start] = part[half:]
                if s > 0:
                    begin = 2 * (slices - s) * HALFCOL + j * COLBLK
                    c = cosine[s, :, begin : begin + COLBLK]
                    d = sine[s, :, begin : begin + COLBLK]
                    parts = operand(c * a + d * b, c * b - d * a)
                    if j > 0:
                        mix_cols(level + 1, j - 1, last, parts, adjoint_cols)
                    last = parts
            yield

    stages = [forward(s) for s in range(slices)] + [residual()] + [backward(s) for s in reversed(range(slices))]
    counts = [blocks - s for s in range(slices)] + [blocks - slices] + [s + 1 for s in reversed(range(slices))]
    order = [(2 * k + t, k) for k, n in enumerate(counts) for t in range(len(pairs(n)))]
    for _, k in sorted(order):
        next(stages[k])


def arrange(sizes, *refs):
    slices, planes = sizes[:2]
    place = lax.axis_index("depth")
    plane = lax.axis_index("row") // 2
    out = refs[-1]
    for k in range(planes):
        for j in range(slices):
            block = (plane ^ k) * slices + (place ^ j)
            out[0, :, pl.ds(pl.multiple_of(block * COLBLK, COLBLK), COLBLK)] = refs[k][j]


def swap(x, axis, step):
    size = lax.axis_size(axis)
    return lax.ppermute(x, axis, [(i, i ^ step) for i in range(size)])


def window_body(index_volume, angles, offsets, measured):
    slices = lax.axis_size("depth")
    planes = lax.axis_size("row") // 2
    place = lax.axis_index("depth")
    core = lax.axis_index("row") % 2
    plane = lax.axis_index("row") // 2
    height, columns = index_volume.shape[1:]
    rows = 2 * planes * height
    half = planes * height
    span = slices * COLBLK
    cone = 2 * slices * HALFCOL
    blocks = 1 + 2 * cone // COLBLK
    width = blocks * COLBLK

    padded = jnp.pad(index_volume[0], ((0, 0), (cone, cone)))
    far = [None] + [
        swap(lax.dynamic_slice_in_dim(padded, span * (plane ^ k), span + 2 * cone, 1), "row", 2 * k)
        for k in range(1, planes)
    ]
    offset_tile = jnp.broadcast_to(offsets[0].astype(jnp.bfloat16), (height, COLBLK))
    near = []
    for j in range(slices):
        part = lax.dynamic_slice_in_dim(padded, span * plane + COLBLK * (place ^ j), width, 1)
        near.append(jnp.concatenate([part, offset_tile], axis=1))
        if j > 0:
            near[j] = swap(near[j], "depth", j)
    far = jnp.stack(far[1:])
    rest = []
    for j in range(slices):
        part = lax.dynamic_slice_in_dim(far, COLBLK * (place ^ j), width, 2)
        rest.append(part if j == 0 else swap(part, "depth", j))
    own = [jnp.concatenate([n[None, :, :width], r]) for n, r in zip(near, rest)]
    own_first = own[0].reshape(1, half, width)
    own_later = jnp.stack(own[1:]).reshape(slices - 1, half, width)
    other = jnp.concatenate([swap(own_first, "row", 1), swap(own_later, "row", 1)])
    own = jnp.concatenate([own_first, own_later])
    tiles = jnp.stack([n[:, width:] for n in near])

    mine = lax.dynamic_index_in_dim(measured, core, 0, False)
    theirs = swap(lax.dynamic_index_in_dim(measured, 1 - core, 0, False), "row", 1)
    both = jnp.pad(jnp.stack([mine, theirs]), ((0, 0), (0, 0), (cone // 2, cone // 2)))
    both, _ = lax.optimization_barrier((both, far))
    seen = [
        lax.dynamic_slice_in_dim(both, span * (plane ^ k) + COLBLK * place, COLBLK + cone, 2) for k in range(planes)
    ]
    seen = jnp.stack([seen[0]] + [swap(seen[k], "row", 2 * k) for k in range(1, planes)])

    sizes = (slices, planes, height, blocks, columns)
    mine, theirs = pl.pallas_call(
        functools.partial(sweep, sizes),
        out_shape=[jax.ShapeDtypeStruct((slices, half, COLBLK), jnp.float32)] * 2,
        in_specs=[pl.BlockSpec(memory_space=pltpu.SMEM)] + [pl.BlockSpec(memory_space=pltpu.VMEM)] * 6,
        out_specs=[pl.BlockSpec(memory_space=pltpu.VMEM)] * 2,
        scratch_shapes=[
            pltpu.VMEM((slices, rows, width), jnp.float32),
            pltpu.VMEM((slices, rows, width), jnp.float32),
            pltpu.VMEM((2 * slices, blocks - 1, rows, 2 * COLBLK), jnp.float32),
            pltpu.VMEM((slices, 2 * rows, COLBLK), jnp.float32),
        ],
        compiler_params=pltpu.CompilerParams(vmem_limit_bytes=40 * 1024 * 1024),
    )(angles, tiles, own, other, seen, jnp.asarray(column_weights(False)), jnp.asarray(column_weights(True)))

    summed = mine + swap(theirs, "row", 1)
    parts = [summed[0]] + [swap(summed[j], "depth", j) for j in range(1, slices)]
    parts = jnp.stack(parts).reshape(slices, planes, height, COLBLK)
    parts = [parts[:, k] if k == 0 else swap(parts[:, k], "row", 2 * k) for k in range(planes)]
    return pl.pallas_call(
        functools.partial(arrange, sizes),
        out_shape=jax.ShapeDtypeStruct((1, height, columns), jnp.float32),
        in_specs=[pl.BlockSpec(memory_space=pltpu.VMEM)] * planes,
        out_specs=pl.BlockSpec(memory_space=pltpu.VMEM),
    )(*parts)


def suits(mesh, index_volume, measured):
    depth, row = mesh.shape["depth"], mesh.shape["row"]
    slices, rows, columns = index_volume.shape
    return (
        slices == depth
        and depth & (depth - 1) == 0
        and row & (row - 1) == 0
        and row > 1
        and measured.shape[0] == 2
        and rows == COLBLK
        and rows // row % 16 == 0
        and columns == COLBLK * depth * (row // 2)
    )


def solution(mesh):
    in_specs = (P("depth", "row", None), P(), P("depth"), P(None, "row", None))
    out_specs = P("depth", "row", None)

    def run(index_volume, angles, offsets, measured):
        chosen = window_body if suits(mesh, index_volume, measured) else body
        mapped = jax.shard_map(chosen, mesh=mesh, in_specs=in_specs, out_specs=out_specs, check_vma=False)
        return mapped(index_volume, angles, offsets, measured)

    return run
```

```python
import functools
import math

import jax
import jax.numpy as jnp
import numpy as np
from jax import lax
from jax.experimental import pallas as pl
from jax.experimental.pallas import tpu as pltpu
from jax.sharding import PartitionSpec as P

TILTS = 16
HALF = 10
SHIFT = 4
HALFCOL = 64
COLBLK = 128


PHASE_SCALE = 0.5
CHIRP_ROW = 1.3
CHIRP_COL = 1.7


def padded_2(shard, sides, width):
    for axis, dim in sides:
        size, length = (lax.axis_size(axis), shard.shape[dim])
        up = [(i, (i + 1) % size) for i in range(size - 1)]
        down = [(j, i) for i, j in up]
        last = lax.slice_in_dim(shard, length - width, length, axis=dim)
        initial = lax.slice_in_dim(shard, 0, width, axis=dim)
        before = lax.ppermute(last, axis, up)
        after = lax.ppermute(initial, axis, down)
        shard = jnp.concatenate([before, shard, after], axis=dim)
    return shard


def from_behind(shard, axis, by):
    length = lax.axis_size(axis)
    pairs = [(i, i + by) for i in range(length) if 0 <= i + by < length]
    return lax.ppermute(shard, axis, pairs)


def kernel_values(distance, radius, chirp_rate):
    inside = jnp.abs(distance) <= radius
    phase_arg = chirp_rate / radius * distance * distance
    weight = 1.0 / math.sqrt(2 * radius + 1)
    real_part = jnp.where(inside, jnp.cos(phase_arg) * weight, 0.0)
    imag_part = jnp.where(inside, jnp.sin(phase_arg) * weight, 0.0)
    return (real_part, imag_part)


def row_band(offset, height, margin, conjugate):
    extent = (height, height + 2 * margin)
    target = lax.broadcasted_iota(jnp.int32, extent, 0)
    source = lax.broadcasted_iota(jnp.int32, extent, 1)
    offset_used = -offset if conjugate else offset
    distance = (source - target - margin - offset_used).astype(jnp.float32)
    real_part, imag_part = kernel_values(distance, HALF, CHIRP_ROW)
    return (real_part, -imag_part) if conjugate else (real_part, imag_part)


def column_band(conjugate, block_width):
    extent = (block_width + 2 * HALFCOL, block_width)
    source = lax.broadcasted_iota(jnp.int32, extent, 0)
    target = lax.broadcasted_iota(jnp.int32, extent, 1)
    distance = (source - target - HALFCOL).astype(jnp.float32)
    real_part, imag_part = kernel_values(distance, HALFCOL, CHIRP_COL)
    return (real_part, -imag_part) if conjugate else (real_part, imag_part)


def mix_rows(band, extended):

    def product(matrix, operand):
        return jnp.einsum("ij,mjc->mic", matrix, operand, precision=lax.Precision.HIGHEST)

    real_part = product(band[0], extended[:, 0]) - product(band[1], extended[:, 1])
    imag_part = product(band[0], extended[:, 1]) + product(band[1], extended[:, 0])
    return jnp.stack([real_part, imag_part], axis=1)


def block_product(window, band):

    def product(operand, matrix):
        return jnp.einsum("mrbj,ji->mrbi", operand, matrix, precision=lax.Precision.HIGHEST)

    real_part = product(window[:, 0], band[0]) - product(window[:, 1], band[1])
    imag_part = product(window[:, 1], band[0]) + product(window[:, 0], band[1])
    return jnp.stack([real_part, imag_part], axis=1)


def mix_columns(band, field):
    amount, _, height, columns = field.shape
    blocks = columns // COLBLK
    padded = jnp.pad(field, ((0, 0), (0, 0), (0, 0), (HALFCOL, COLBLK - HALFCOL)))
    middle = padded[..., :columns].reshape(amount, 2, height, blocks, COLBLK)
    beyond = padded[..., COLBLK : columns + COLBLK].reshape(amount, 2, height, blocks, COLBLK)
    window = jnp.concatenate([middle, beyond], axis=4)
    return block_product(window, band).reshape(amount, 2, height, columns)


def rotate(field, cosine, sine):
    real_part = cosine * field[:, 0] - sine * field[:, 1]
    imag_part = cosine * field[:, 1] + sine * field[:, 0]
    return jnp.stack([real_part, imag_part], axis=1)


def slab_forward(field, index_volume, offsets, active):
    margin = HALF + SHIFT
    height = field.shape[2]
    col_band = column_band(False, COLBLK)
    phase_arg = PHASE_SCALE * index_volume[0].astype(jnp.float32)
    transmitted = rotate(field, jnp.cos(phase_arg), jnp.sin(phase_arg))
    stored_fields = [transmitted]
    extended = padded_2(transmitted, (("row", 2),), margin)
    band = row_band(offsets[0], height, margin, False)

    def advance(operand, band=band):
        return mix_columns(col_band, mix_rows(band, operand))

    def remain(operand):
        return operand[:, :, margin : margin + height, :]

    field = lax.cond(active, advance, remain, extended)
    return (field, jnp.stack(stored_fields, axis=0))


def slab_adjoint(adjoint, stored, index_volume, offsets, active):
    margin = HALF + SHIFT
    height = adjoint.shape[2]
    col_band = column_band(True, COLBLK)
    layers = index_volume.shape[0]
    slab_grads = [None] * layers

    def column_step(operand):
        return mix_columns(col_band, operand)

    def unchanged(operand):
        return operand

    def remain(operand):
        return operand[:, :, margin : margin + height, :]

    for layer_no in reversed(range(layers)):
        returned = lax.cond(active, column_step, unchanged, adjoint)
        extended = padded_2(returned, (("row", 2),), margin)
        band = row_band(offsets[layer_no], height, margin, True)

        def row_step(operand, band=band):
            return mix_rows(band, operand)

        returned = lax.cond(active, row_step, remain, extended)
        transmitted = stored[layer_no]
        slab_grads[layer_no] = PHASE_SCALE * jnp.sum(
            transmitted[:, 0] * returned[:, 1] - transmitted[:, 1] * returned[:, 0], axis=0
        )
        phase_arg = PHASE_SCALE * index_volume[layer_no].astype(jnp.float32)
        adjoint = rotate(returned, jnp.cos(phase_arg), -jnp.sin(phase_arg))
    return (adjoint, jnp.stack(slab_grads, axis=0))


def plane_waves(angles, row_start, height, columns, total_rows, total_cols):
    across = angles - TILTS // 2
    along = jnp.mod(3 * angles, TILTS) - TILTS // 2
    row_index = row_start + lax.broadcasted_iota(jnp.int32, (height, columns), 0)
    col_index = lax.broadcasted_iota(jnp.int32, (height, columns), 1)
    period = total_cols * total_rows
    cycles_int = jnp.mod(
        across[:, None, None] * col_index[None] * total_rows
        + along[:, None, None] * row_index[None] * total_cols,
        period,
    )
    phase_arg = 2.0 * math.pi / period * cycles_int.astype(jnp.float32)
    return jnp.stack([jnp.cos(phase_arg), jnp.sin(phase_arg)], axis=1)


def body(index_volume, angles, offsets, measured):
    sections = lax.axis_size("depth")
    section_no = lax.axis_index("depth")
    number = angles.shape[0]
    layers = index_volume.shape[0]
    height = index_volume.shape[1]
    columns = index_volume.shape[2]
    row_start = lax.axis_index("row") * height
    total_rows = height * lax.axis_size("row")
    intensity = measured.astype(jnp.float32)
    grad_init = jnp.zeros((layers, height, columns), jnp.float32)
    incident = plane_waves(angles, row_start, height, columns, total_rows, columns)
    kept_init = jnp.zeros((layers,) + incident.shape, jnp.float32)

    def forward_compute(counter, received, stored, exit_field):
        angle_no = counter - section_no
        active = (angle_no >= 0) & (angle_no < number)
        chosen = jnp.clip(angle_no, 0, number - 1)
        entering = jnp.where(
            section_no == 0, lax.dynamic_slice_in_dim(incident, chosen, 1, 0), received
        )
        result, kept = slab_forward(entering, index_volume, offsets, active)
        placed_kept = lax.dynamic_update_slice_in_dim(stored, kept, chosen, 1)
        stored = jnp.where(active, placed_kept, stored)
        placed = lax.dynamic_update_slice_in_dim(exit_field, result, chosen, 0)
        exit_field = jnp.where(active, placed, exit_field)
        return (result, stored, exit_field)

    def forward_turn(counter, carried):
        result, stored, exit_field = forward_compute(counter, carried[0], carried[1], carried[2])
        return (from_behind(result, "depth", 1), stored, exit_field)

    zero_single = jnp.zeros((1,) + incident.shape[1:], jnp.float32)
    turns = sections + number - 1
    received, stored, exit_field = lax.fori_loop(
        0, turns - 1, forward_turn, (zero_single, kept_init, jnp.zeros_like(incident))
    )
    leftover, stored, exit_field = forward_compute(turns - 1, received, stored, exit_field)
    errors = exit_field[:, 0] * exit_field[:, 0] + exit_field[:, 1] * exit_field[:, 1] - intensity
    exit_adjoint = 2.0 * errors[:, None] * exit_field

    def backward_compute(counter, received, gradient):
        angle_no = counter - (sections - 1 - section_no)
        active = (angle_no >= 0) & (angle_no < number)
        chosen = jnp.clip(angle_no, 0, number - 1)
        entering = jnp.where(
            section_no == sections - 1,
            lax.dynamic_slice_in_dim(exit_adjoint, chosen, 1, 0),
            received,
        )
        result, slab_terms = slab_adjoint(
            entering, lax.dynamic_slice_in_dim(stored, chosen, 1, 1), index_volume, offsets, active
        )
        return (result, jnp.where(active, gradient + slab_terms, gradient))

    def backward_turn(counter, carried):
        result, gradient = backward_compute(counter, carried[0], carried[1])
        return (from_behind(result, "depth", -1), gradient)

    received, gradient = lax.fori_loop(0, turns - 1, backward_turn, (zero_single, grad_init))
    leftover, gradient = backward_compute(turns - 1, received, gradient)
    return gradient


def taps_of(radius, chirp_rate):
    distance = np.arange(-radius, radius + 1, dtype=np.float64)
    phase_arg = chirp_rate / radius * distance * distance
    weight = 1.0 / math.sqrt(2 * radius + 1)
    return (np.cos(phase_arg) * weight, np.sin(phase_arg) * weight)


def column_parts():
    taps = taps_of(HALFCOL, CHIRP_COL)
    source = np.arange(COLBLK + 2 * HALFCOL)[:, None]
    target = np.arange(COLBLK)[None, :]
    place = source - target
    inside = (place >= 0) & (place <= 2 * HALFCOL)
    parts = [np.where(inside, t[np.clip(place, 0, 2 * HALFCOL)], 0.0) for t in taps]
    high = [part.astype(jnp.bfloat16) for part in parts]
    low = [(part - h.astype(np.float64)).astype(jnp.bfloat16) for part, h in zip(parts, high)]
    return [[jnp.asarray(part) for part in pair] for pair in (high, low)]


def column_weights(high, low):
    results = []
    for sign in (1, -1):
        rows = []
        for real_part, imag_part in (high, low):
            rows.append(jnp.concatenate([real_part, sign * imag_part], axis=1))
            rows.append(jnp.concatenate([-sign * imag_part, real_part], axis=1))
        results.append(jnp.concatenate(rows))
    return results


def series(kind):
    nodes = np.cos((np.arange(40) + 0.5) * np.pi / 40) * 8.0 + 8.0
    x = np.sqrt(nodes)
    values = np.cos(PHASE_SCALE * x) if kind == "cos" else np.sin(PHASE_SCALE * x) / x
    fitted = np.polynomial.chebyshev.Chebyshev.fit(nodes, values, 6, domain=[0.0, 16.0])
    return [float(v) for v in fitted.convert(kind=np.polynomial.Polynomial).coef]


COS_SERIES = series("cos")
SIN_SERIES = series("sin")


def evaluate(coefficients, x):
    total = x * coefficients[-1] + coefficients[-2]
    for value in coefficients[-3::-1]:
        total = total * x + value
    return total


def split(x):
    high = x.astype(jnp.bfloat16)
    return (high, (x - high.astype(jnp.float32)).astype(jnp.bfloat16))


def dot(a, b):
    return jnp.dot(a, b, preferred_element_type=jnp.float32)


def row_factor(rows_of, rows_across, offset):
    n = rows_of.shape[0]
    distance = jnp.abs(rows_across - rows_of - offset)
    cosines, sines = taps_of(HALF, CHIRP_ROW)
    real_part = jnp.zeros((n, n), jnp.float32)
    imag_part = jnp.zeros((n, n), jnp.float32)
    for k in range(HALF + 1):
        hit = distance == k
        real_part = jnp.where(hit, float(cosines[HALF + k]), real_part)
        imag_part = jnp.where(hit, float(sines[HALF + k]), imag_part)
    return (real_part, imag_part)


def complex_form(real_part, imag_part):
    upper = jnp.concatenate([real_part, -imag_part], axis=1)
    lower = jnp.concatenate([imag_part, real_part], axis=1)
    return jnp.concatenate([upper, lower], axis=0)


def sweep(sizes, tilts, tiles, own, other, measured, forward_cols, adjoint_cols, mine, theirs, cosine, sine, field, kept):
    slices, planes, height, blocks, broad, columns = sizes
    half = planes * height
    rows = 2 * half
    place = lax.axis_index("depth")
    core = lax.axis_index("row") % 2
    plane = lax.axis_index("row") // 2
    block = plane % 2 * slices + place
    across, along = [jnp.where(core == 0, tilts[i : i + 1, :1], tilts[i : i + 1, 1:]) for i in range(2)]

    def row_numbers(axis):
        i = lax.broadcasted_iota(jnp.int32, (rows, rows), axis)
        side = i // half
        step = (i - side * half) // height
        return 2 * height * (plane ^ step) + height * (core ^ side) + i % height

    rows_of, rows_across = row_numbers(0), row_numbers(1)
    walk_off = [tiles[place ^ s, :1].astype(jnp.int32) for s in range(slices)]
    factors = [row_factor(rows_of, rows_across, offset) for offset in walk_off]
    width = blocks * COLBLK
    first = block * broad - 2 * slices * HALFCOL
    lane = first + lax.broadcasted_iota(jnp.int32, (1, width), 1)
    inside = (lane >= 0) & (lane < columns)

    turn = 2.0 * math.pi / columns
    col_phase = turn * (lax.rem(across * lane, columns)).astype(jnp.float32)
    row_phase = 2.0 * math.pi / rows * (lax.rem(along * row_numbers(0)[:, :1], rows)).astype(jnp.float32)
    row_cos, row_sin = jnp.cos(row_phase), jnp.sin(row_phase)
    col_cos, col_sin = jnp.cos(col_phase), jnp.sin(col_phase)

    def read(level, j):
        return (field[level, j, :, :COLBLK], field[level, j, :, COLBLK:])

    def operand(a, b):
        a_high, a_low = split(a)
        b_high, b_low = split(b)
        return (a_high, b_high, a_low, b_low)

    def mix_cols(level, j, left, right, weights):
        wide = jnp.concatenate([part for pair in zip(left, right) for part in pair], axis=1)
        high, low = wide[:, : 4 * COLBLK], wide[:, 4 * COLBLK :]
        total = dot(high, weights[: 4 * COLBLK]) + (dot(low, weights[: 4 * COLBLK]) + dot(high, weights[4 * COLBLK :]))
        field[level, j] = total

    def mix_rows(factor, blocks_in):
        y = jnp.concatenate([jnp.concatenate([a, b], axis=0) for a, b in blocks_in], axis=1)
        y_high, y_low = split(y)
        v = dot(factor[0], y_high) + (dot(factor[0], y_low) + dot(factor[1], y_high))
        cut = [slice(i * COLBLK, (i + 1) * COLBLK) for i in range(len(blocks_in))]
        return [(v[:rows, c], v[rows:, c]) for c in cut]

    def pairs(n):
        return [range(j, min(j + 2, n)) for j in range(0, n, 2)]

    def forward(s):
        factor = split(complex_form(*factors[s]))
        slot = place ^ s
        last = None
        for group in pairs(blocks - s):
            turned = []
            for j in group:
                begin = s * HALFCOL + j * COLBLK
                x = jnp.concatenate([r[slot, :, begin : begin + COLBLK] for r in (own, other)], axis=0)
                x = x.astype(jnp.float32)
                square = x * x
                seen = inside[:, begin : begin + COLBLK]
                c = jnp.where(seen, evaluate(COS_SERIES, square), 0.0)
                d = jnp.where(seen, evaluate(SIN_SERIES, square) * x, 0.0)
                if s > 0:
                    cosine[s, :, j * COLBLK : (j + 1) * COLBLK] = c
                    sine[s, :, j * COLBLK : (j + 1) * COLBLK] = d
                if s == 0:
                    cc, cs = col_cos[:, begin : begin + COLBLK], col_sin[:, begin : begin + COLBLK]
                    a = row_cos * cc - row_sin * cs
                    b = row_cos * cs + row_sin * cc
                else:
                    a, b = read(s - 1, j)
                a, b = c * a - d * b, c * b + d * a
                start = (2 * slices - s) * HALFCOL - j * COLBLK
                lo, hi = max(start, 0), min(start + broad, COLBLK)
                if lo < hi:
                    kept[s, :rows, lo - start : hi - start] = a[:, lo:hi]
                    kept[s, rows:, lo - start : hi - start] = b[:, lo:hi]
                turned.append((a, b))
            for j, v in zip(group, mix_rows(factor, turned)):
                parts = operand(*v)
                if j > 0:
                    mix_cols(s, j - 1, last, parts, forward_cols)
                last = parts
            yield

    def residual():
        last = None
        for group in pairs(blocks - slices):
            for j in group:
                a, b = read(slices - 1, j)
                cols = slice(j * COLBLK, (j + 1) * COLBLK)
                seen = [measured[k, side, :, cols] for side in range(2) for k in range(planes)]
                seen = jnp.concatenate(seen, axis=0).astype(jnp.float32)
                begin = slices * HALFCOL + j * COLBLK
                error = 2.0 * (a * a + b * b - seen)
                error = jnp.where(inside[:, begin : begin + COLBLK], error, 0.0)
                parts = operand(error * a, error * b)
                if j > 0:
                    mix_cols(slices, j - 1, last, parts, adjoint_cols)
                last = parts
            yield

    def backward(s):
        real_part, imag_part = factors[s]
        factor = split(complex_form(real_part.T, -imag_part.T))
        level = 2 * slices - 1 - s
        last = None
        for group in pairs(s + broad // COLBLK):
            for j, (a, b) in zip(group, mix_rows(factor, [read(level, j) for j in group])):
                start = s * HALFCOL - j * COLBLK
                lo, hi = max(start, 0), min(start + broad, COLBLK)
                if lo < hi:
                    y = kept[s, :, lo - start : hi - start]
                    part = PHASE_SCALE * (y[:rows] * b[:, lo:hi] - y[rows:] * a[:, lo:hi])
                    mine[place ^ s, :, lo - start : hi - start] = part[: 2 * height]
                    theirs[place ^ s, :, lo - start : hi - start] = part[half : half + 2 * height]
                if s > 0:
                    begin = 2 * (slices - s) * HALFCOL + j * COLBLK
                    c = cosine[s, :, begin : begin + COLBLK]
                    d = sine[s, :, begin : begin + COLBLK]
                    parts = operand(c * a + d * b, c * b - d * a)
                    if j > 0:
                        mix_cols(level + 1, j - 1, last, parts, adjoint_cols)
                    last = parts
            yield

    stages = [forward(s) for s in range(slices)] + [residual()] + [backward(s) for s in reversed(range(slices))]
    counts = [blocks - s for s in range(slices)] + [blocks - slices] + [s + broad // COLBLK for s in reversed(range(slices))]
    order = [(2 * k + t, k) for k, n in enumerate(counts) for t in range(len(pairs(n)))]
    for _, k in sorted(order):
        next(stages[k])


def arrange(sizes, *refs):
    slices, broad = sizes[0], sizes[4]
    place = lax.axis_index("depth")
    group = lax.axis_index("row") // 2 % 2
    out = refs[-1]
    for j in range(slices):
        for i in range(2):
            block = (group ^ i) * slices + (place ^ j)
            out[0, :, pl.ds(pl.multiple_of(block * broad, broad), broad)] = refs[j][i]


def swap(x, axis, step):
    size = lax.axis_size(axis)
    return lax.ppermute(x, axis, [(i, i ^ step) for i in range(size)])


def window_body(index_volume, angles, offsets, measured):
    slices = lax.axis_size("depth")
    planes = lax.axis_size("row") // 2
    place = lax.axis_index("depth")
    core = lax.axis_index("row") % 2
    plane = lax.axis_index("row") // 2
    group = plane % 2
    height, columns = index_volume.shape[1:]
    rows = 2 * planes * height
    half = planes * height
    span = columns // 2
    broad = span // slices
    cone = 2 * slices * HALFCOL
    blocks = (broad + 2 * cone) // COLBLK
    width = blocks * COLBLK

    mine = lax.dynamic_index_in_dim(measured, core, 0, False)
    theirs = swap(lax.dynamic_index_in_dim(measured, 1 - core, 0, False), "row", 1)
    both = jnp.pad(jnp.stack([mine, theirs]), ((0, 0), (0, 0), (cone // 2, cone // 2)))
    first_two = [lax.dynamic_slice_in_dim(both, span * (group ^ i) + broad * place, broad + cone, 2) for i in range(2)]
    weights, first_two = lax.optimization_barrier((column_parts(), first_two))

    far = [
        lax.dynamic_slice_in_dim(index_volume[0], (span - cone) * (group ^ k % 2), span + cone, 1)
        for k in range(planes)
    ]
    far = [far[k] if k == 0 else swap(far[k], "row", 2 * k) for k in range(planes)]
    tilts = jnp.stack([angles - TILTS // 2, jnp.mod(3 * angles, TILTS) - TILTS // 2])
    weights, tilts, first_two, far = lax.optimization_barrier(
        (column_weights(*weights), tilts, first_two, far)
    )
    far = jnp.pad(jnp.stack(far), ((0, 0), (0, 0), (cone, cone)))
    offset_tile = jnp.broadcast_to(offsets[0].astype(jnp.bfloat16), (planes, height, COLBLK))
    parts = [lax.dynamic_slice_in_dim(far, cone * group + broad * (place ^ j), width, 2) for j in range(slices)]
    own = [jnp.concatenate([part, offset_tile], axis=2) for part in parts]
    last_sent = own[1]
    own = [own[j] if j == 0 else swap(own[j], "depth", j) for j in range(slices)]
    tiles = jnp.stack([x[0, :, width:] for x in own])
    own_first = own[0][:, :, :width].reshape(1, half, width)
    own_later = jnp.stack([x[:, :, :width] for x in own[1:]]).reshape(slices - 1, half, width)
    other_first = swap(own_first, "row", 1)
    other = jnp.concatenate([other_first, swap(own_later, "row", 1)])
    own = jnp.concatenate([own_first, own_later])

    first_two = jnp.stack([first_two[0], swap(first_two[1], "row", 2)])
    first_two, _ = lax.optimization_barrier((first_two, last_sent))
    seen = [first_two] + [swap(first_two, "row", 2 * k) for k in range(2, planes, 2)]
    seen = jnp.concatenate(seen)

    sizes = (slices, planes, height, blocks, broad, columns)
    mine, theirs = pl.pallas_call(
        functools.partial(sweep, sizes),
        out_shape=[jax.ShapeDtypeStruct((slices, 2 * height, broad), jnp.float32)] * 2,
        in_specs=[pl.BlockSpec(memory_space=pltpu.VMEM)] * 7,
        out_specs=[pl.BlockSpec(memory_space=pltpu.VMEM)] * 2,
        scratch_shapes=[
            pltpu.VMEM((slices, rows, width), jnp.float32),
            pltpu.VMEM((slices, rows, width), jnp.float32),
            pltpu.VMEM((2 * slices, blocks - 1, rows, 2 * COLBLK), jnp.float32),
            pltpu.VMEM((slices, 2 * rows, broad), jnp.float32),
        ],
        compiler_params=pltpu.CompilerParams(vmem_limit_bytes=40 * 1024 * 1024),
    )(tilts, tiles, own, other, seen, *weights)

    summed = mine + swap(theirs, "row", 1)
    parts = jnp.stack([summed[:, :height], swap(summed[:, height:], "row", 2)], axis=1)
    parts = [parts[j] if j == 0 else swap(parts[j], "depth", j) for j in range(slices)]
    return pl.pallas_call(
        functools.partial(arrange, sizes),
        out_shape=jax.ShapeDtypeStruct((1, height, columns), jnp.float32),
        in_specs=[pl.BlockSpec(memory_space=pltpu.VMEM)] * slices,
        out_specs=pl.BlockSpec(memory_space=pltpu.VMEM),
        compiler_params=pltpu.CompilerParams(vmem_limit_bytes=4 * 1024 * 1024),
    )(*parts)


def suits(mesh, index_volume, measured):
    depth, row = mesh.shape["depth"], mesh.shape["row"]
    slices, rows, columns = index_volume.shape
    return (
        slices == depth
        and depth & (depth - 1) == 0
        and row & (row - 1) == 0
        and row > 2
        and measured.shape[0] == 2
        and rows == COLBLK
        and rows // row % 16 == 0
        and columns % (2 * depth * COLBLK) == 0
        and columns >= 4 * depth * HALFCOL
    )


def solution(mesh):
    in_specs = (P("depth", "row", None), P(), P("depth"), P(None, "row", None))
    out_specs = P("depth", "row", None)

    def run(index_volume, angles, offsets, measured):
        chosen = window_body if suits(mesh, index_volume, measured) else body
        mapped = jax.shard_map(chosen, mesh=mesh, in_specs=in_specs, out_specs=out_specs, check_vma=False)
        return mapped(index_volume, angles, offsets, measured)

    return run
```

```python
import functools
import math

import jax
import jax.numpy as jnp
import numpy as np
from jax import lax
from jax.experimental import pallas as pl
from jax.experimental.pallas import tpu as pltpu
from jax.sharding import PartitionSpec as P

TILTS = 16
HALF = 10
SHIFT = 4
HALFCOL = 64
COLBLK = 128


PHASE_SCALE = 0.5
CHIRP_ROW = 1.3
CHIRP_COL = 1.7


def padded_2(shard, sides, width):
    for axis, dim in sides:
        size, length = (lax.axis_size(axis), shard.shape[dim])
        up = [(i, (i + 1) % size) for i in range(size - 1)]
        down = [(j, i) for i, j in up]
        last = lax.slice_in_dim(shard, length - width, length, axis=dim)
        initial = lax.slice_in_dim(shard, 0, width, axis=dim)
        before = lax.ppermute(last, axis, up)
        after = lax.ppermute(initial, axis, down)
        shard = jnp.concatenate([before, shard, after], axis=dim)
    return shard


def from_behind(shard, axis, by):
    length = lax.axis_size(axis)
    pairs = [(i, i + by) for i in range(length) if 0 <= i + by < length]
    return lax.ppermute(shard, axis, pairs)


def kernel_values(distance, radius, chirp_rate):
    inside = jnp.abs(distance) <= radius
    phase_arg = chirp_rate / radius * distance * distance
    weight = 1.0 / math.sqrt(2 * radius + 1)
    real_part = jnp.where(inside, jnp.cos(phase_arg) * weight, 0.0)
    imag_part = jnp.where(inside, jnp.sin(phase_arg) * weight, 0.0)
    return (real_part, imag_part)


def row_band(offset, height, margin, conjugate):
    extent = (height, height + 2 * margin)
    target = lax.broadcasted_iota(jnp.int32, extent, 0)
    source = lax.broadcasted_iota(jnp.int32, extent, 1)
    offset_used = -offset if conjugate else offset
    distance = (source - target - margin - offset_used).astype(jnp.float32)
    real_part, imag_part = kernel_values(distance, HALF, CHIRP_ROW)
    return (real_part, -imag_part) if conjugate else (real_part, imag_part)


def column_band(conjugate, block_width):
    extent = (block_width + 2 * HALFCOL, block_width)
    source = lax.broadcasted_iota(jnp.int32, extent, 0)
    target = lax.broadcasted_iota(jnp.int32, extent, 1)
    distance = (source - target - HALFCOL).astype(jnp.float32)
    real_part, imag_part = kernel_values(distance, HALFCOL, CHIRP_COL)
    return (real_part, -imag_part) if conjugate else (real_part, imag_part)


def mix_rows(band, extended):

    def product(matrix, operand):
        return jnp.einsum("ij,mjc->mic", matrix, operand, precision=lax.Precision.HIGHEST)

    real_part = product(band[0], extended[:, 0]) - product(band[1], extended[:, 1])
    imag_part = product(band[0], extended[:, 1]) + product(band[1], extended[:, 0])
    return jnp.stack([real_part, imag_part], axis=1)


def block_product(window, band):

    def product(operand, matrix):
        return jnp.einsum("mrbj,ji->mrbi", operand, matrix, precision=lax.Precision.HIGHEST)

    real_part = product(window[:, 0], band[0]) - product(window[:, 1], band[1])
    imag_part = product(window[:, 1], band[0]) + product(window[:, 0], band[1])
    return jnp.stack([real_part, imag_part], axis=1)


def mix_columns(band, field):
    amount, _, height, columns = field.shape
    blocks = columns // COLBLK
    padded = jnp.pad(field, ((0, 0), (0, 0), (0, 0), (HALFCOL, COLBLK - HALFCOL)))
    middle = padded[..., :columns].reshape(amount, 2, height, blocks, COLBLK)
    beyond = padded[..., COLBLK : columns + COLBLK].reshape(amount, 2, height, blocks, COLBLK)
    window = jnp.concatenate([middle, beyond], axis=4)
    return block_product(window, band).reshape(amount, 2, height, columns)


def rotate(field, cosine, sine):
    real_part = cosine * field[:, 0] - sine * field[:, 1]
    imag_part = cosine * field[:, 1] + sine * field[:, 0]
    return jnp.stack([real_part, imag_part], axis=1)


def slab_forward(field, index_volume, offsets, active):
    margin = HALF + SHIFT
    height = field.shape[2]
    col_band = column_band(False, COLBLK)
    phase_arg = PHASE_SCALE * index_volume[0].astype(jnp.float32)
    transmitted = rotate(field, jnp.cos(phase_arg), jnp.sin(phase_arg))
    stored_fields = [transmitted]
    extended = padded_2(transmitted, (("row", 2),), margin)
    band = row_band(offsets[0], height, margin, False)

    def advance(operand, band=band):
        return mix_columns(col_band, mix_rows(band, operand))

    def remain(operand):
        return operand[:, :, margin : margin + height, :]

    field = lax.cond(active, advance, remain, extended)
    return (field, jnp.stack(stored_fields, axis=0))


def slab_adjoint(adjoint, stored, index_volume, offsets, active):
    margin = HALF + SHIFT
    height = adjoint.shape[2]
    col_band = column_band(True, COLBLK)
    layers = index_volume.shape[0]
    slab_grads = [None] * layers

    def column_step(operand):
        return mix_columns(col_band, operand)

    def unchanged(operand):
        return operand

    def remain(operand):
        return operand[:, :, margin : margin + height, :]

    for layer_no in reversed(range(layers)):
        returned = lax.cond(active, column_step, unchanged, adjoint)
        extended = padded_2(returned, (("row", 2),), margin)
        band = row_band(offsets[layer_no], height, margin, True)

        def row_step(operand, band=band):
            return mix_rows(band, operand)

        returned = lax.cond(active, row_step, remain, extended)
        transmitted = stored[layer_no]
        slab_grads[layer_no] = PHASE_SCALE * jnp.sum(
            transmitted[:, 0] * returned[:, 1] - transmitted[:, 1] * returned[:, 0], axis=0
        )
        phase_arg = PHASE_SCALE * index_volume[layer_no].astype(jnp.float32)
        adjoint = rotate(returned, jnp.cos(phase_arg), -jnp.sin(phase_arg))
    return (adjoint, jnp.stack(slab_grads, axis=0))


def plane_waves(angles, row_start, height, columns, total_rows, total_cols):
    across = angles - TILTS // 2
    along = jnp.mod(3 * angles, TILTS) - TILTS // 2
    row_index = row_start + lax.broadcasted_iota(jnp.int32, (height, columns), 0)
    col_index = lax.broadcasted_iota(jnp.int32, (height, columns), 1)
    period = total_cols * total_rows
    cycles_int = jnp.mod(
        across[:, None, None] * col_index[None] * total_rows
        + along[:, None, None] * row_index[None] * total_cols,
        period,
    )
    phase_arg = 2.0 * math.pi / period * cycles_int.astype(jnp.float32)
    return jnp.stack([jnp.cos(phase_arg), jnp.sin(phase_arg)], axis=1)


def body(index_volume, angles, offsets, measured):
    sections = lax.axis_size("depth")
    section_no = lax.axis_index("depth")
    number = angles.shape[0]
    layers = index_volume.shape[0]
    height = index_volume.shape[1]
    columns = index_volume.shape[2]
    row_start = lax.axis_index("row") * height
    total_rows = height * lax.axis_size("row")
    intensity = measured.astype(jnp.float32)
    grad_init = jnp.zeros((layers, height, columns), jnp.float32)
    incident = plane_waves(angles, row_start, height, columns, total_rows, columns)
    kept_init = jnp.zeros((layers,) + incident.shape, jnp.float32)

    def forward_compute(counter, received, stored, exit_field):
        angle_no = counter - section_no
        active = (angle_no >= 0) & (angle_no < number)
        chosen = jnp.clip(angle_no, 0, number - 1)
        entering = jnp.where(
            section_no == 0, lax.dynamic_slice_in_dim(incident, chosen, 1, 0), received
        )
        result, kept = slab_forward(entering, index_volume, offsets, active)
        placed_kept = lax.dynamic_update_slice_in_dim(stored, kept, chosen, 1)
        stored = jnp.where(active, placed_kept, stored)
        placed = lax.dynamic_update_slice_in_dim(exit_field, result, chosen, 0)
        exit_field = jnp.where(active, placed, exit_field)
        return (result, stored, exit_field)

    def forward_turn(counter, carried):
        result, stored, exit_field = forward_compute(counter, carried[0], carried[1], carried[2])
        return (from_behind(result, "depth", 1), stored, exit_field)

    zero_single = jnp.zeros((1,) + incident.shape[1:], jnp.float32)
    turns = sections + number - 1
    received, stored, exit_field = lax.fori_loop(
        0, turns - 1, forward_turn, (zero_single, kept_init, jnp.zeros_like(incident))
    )
    leftover, stored, exit_field = forward_compute(turns - 1, received, stored, exit_field)
    errors = exit_field[:, 0] * exit_field[:, 0] + exit_field[:, 1] * exit_field[:, 1] - intensity
    exit_adjoint = 2.0 * errors[:, None] * exit_field

    def backward_compute(counter, received, gradient):
        angle_no = counter - (sections - 1 - section_no)
        active = (angle_no >= 0) & (angle_no < number)
        chosen = jnp.clip(angle_no, 0, number - 1)
        entering = jnp.where(
            section_no == sections - 1,
            lax.dynamic_slice_in_dim(exit_adjoint, chosen, 1, 0),
            received,
        )
        result, slab_terms = slab_adjoint(
            entering, lax.dynamic_slice_in_dim(stored, chosen, 1, 1), index_volume, offsets, active
        )
        return (result, jnp.where(active, gradient + slab_terms, gradient))

    def backward_turn(counter, carried):
        result, gradient = backward_compute(counter, carried[0], carried[1])
        return (from_behind(result, "depth", -1), gradient)

    received, gradient = lax.fori_loop(0, turns - 1, backward_turn, (zero_single, grad_init))
    leftover, gradient = backward_compute(turns - 1, received, gradient)
    return gradient


def taps_of(radius, chirp_rate):
    distance = np.arange(-radius, radius + 1, dtype=np.float64)
    phase_arg = chirp_rate / radius * distance * distance
    weight = 1.0 / math.sqrt(2 * radius + 1)
    return (np.cos(phase_arg) * weight, np.sin(phase_arg) * weight)


def column_parts():
    taps = taps_of(HALFCOL, CHIRP_COL)
    source = np.arange(COLBLK + 2 * HALFCOL)[:, None]
    target = np.arange(COLBLK)[None, :]
    place = source - target
    inside = (place >= 0) & (place <= 2 * HALFCOL)
    parts = [np.where(inside, t[np.clip(place, 0, 2 * HALFCOL)], 0.0) for t in taps]
    high = [part.astype(jnp.bfloat16) for part in parts]
    low = [(part - h.astype(np.float64)).astype(jnp.bfloat16) for part, h in zip(parts, high)]
    return [[jnp.asarray(part) for part in pair] for pair in (high, low)]


def column_weights(high, low):
    results = []
    for sign in (1, -1):
        rows = []
        for real_part, imag_part in (high, low):
            rows.append(jnp.concatenate([real_part, sign * imag_part], axis=1))
            rows.append(jnp.concatenate([-sign * imag_part, real_part], axis=1))
        results.append(jnp.concatenate(rows))
    return results


def series(kind, degree):
    nodes = np.cos((np.arange(40) + 0.5) * np.pi / 40) * 8.0 + 8.0
    x = np.sqrt(nodes)
    values = np.cos(PHASE_SCALE * x) if kind == "cos" else np.sin(PHASE_SCALE * x) / x
    fitted = np.polynomial.chebyshev.Chebyshev.fit(nodes, values, degree, domain=[0.0, 16.0])
    return [float(v) for v in fitted.convert(kind=np.polynomial.Polynomial).coef]


COS_SERIES = series("cos", 5)
SIN_SERIES = series("sin", 5)


def evaluate(coefficients, x):
    total = x * coefficients[-1] + coefficients[-2]
    for value in coefficients[-3::-1]:
        total = total * x + value
    return total


def split(x):
    high = x.astype(jnp.bfloat16)
    return (high, (x - high.astype(jnp.float32)).astype(jnp.bfloat16))


def dot(a, b):
    return jnp.dot(a, b, preferred_element_type=jnp.float32)


def row_factor(rows_of, rows_across, offset):
    n = rows_of.shape[0]
    distance = jnp.abs(rows_across - rows_of - offset)
    cosines, sines = taps_of(HALF, CHIRP_ROW)
    real_part = jnp.zeros((n, n), jnp.float32)
    imag_part = jnp.zeros((n, n), jnp.float32)
    for k in range(HALF + 1):
        hit = distance == k
        real_part = jnp.where(hit, float(cosines[HALF + k]), real_part)
        imag_part = jnp.where(hit, float(sines[HALF + k]), imag_part)
    return (real_part, imag_part)


def complex_form(real_part, imag_part):
    upper = jnp.concatenate([real_part, -imag_part], axis=1)
    lower = jnp.concatenate([imag_part, real_part], axis=1)
    return jnp.concatenate([upper, lower], axis=0)


def sweep(sizes, tilts, tiles, own, other, measured, forward_cols, adjoint_cols, mine, theirs, cosine, sine, field, kept):
    slices, planes, height, blocks, broad, columns = sizes
    half = planes * height
    rows = 2 * half
    place = lax.axis_index("depth")
    core = lax.axis_index("row") % 2
    plane = lax.axis_index("row") // 2
    block = plane % 2 * slices + place
    across, along = [jnp.where(core == 0, tilts[i : i + 1, :1], tilts[i : i + 1, 1:]) for i in range(2)]

    def row_numbers(axis):
        i = lax.broadcasted_iota(jnp.int32, (rows, rows), axis)
        side = i // half
        step = (i - side * half) // height
        return 2 * height * (plane ^ step) + height * (core ^ side) + i % height

    rows_of, rows_across = row_numbers(0), row_numbers(1)
    walk_off = [tiles[place ^ s, :1].astype(jnp.int32) for s in range(slices)]
    factors = [row_factor(rows_of, rows_across, offset) for offset in walk_off]
    width = blocks * COLBLK
    first = block * broad - 2 * slices * HALFCOL
    lane = first + lax.broadcasted_iota(jnp.int32, (1, width), 1)
    inside = (lane >= 0) & (lane < columns)

    def wave(count, period):
        count = lax.rem(count, period)
        count = jnp.where(2 * count >= period, count - period, count)
        count = jnp.where(2 * count < -period, count + period, count)
        x = 2.0 * math.pi / period * count.astype(jnp.float32)
        c = evaluate(COS_SERIES, x * x)
        d = evaluate(SIN_SERIES, x * x) * x
        return (1.0 - 2.0 * d * d, 2.0 * c * d)

    row_cos, row_sin = wave(along * row_numbers(0)[:, :1], rows)
    col_cos, col_sin = wave(across * lane, columns)

    def read(level, j):
        return (field[level, j, :, :COLBLK], field[level, j, :, COLBLK:])

    def operand(a, b):
        a_high, a_low = split(a)
        b_high, b_low = split(b)
        return (a_high, b_high, a_low, b_low)

    def mix_cols(level, j, left, right, weights):
        wide = jnp.concatenate([part for pair in zip(left, right) for part in pair], axis=1)
        high, low = wide[:, : 4 * COLBLK], wide[:, 4 * COLBLK :]
        total = dot(high, weights[: 4 * COLBLK]) + (dot(low, weights[: 4 * COLBLK]) + dot(high, weights[4 * COLBLK :]))
        field[level, j] = total

    def mix_rows(factor, blocks_in):
        y = jnp.concatenate([jnp.concatenate([a, b], axis=0) for a, b in blocks_in], axis=1)
        y_high, y_low = split(y)
        v = dot(factor[0], y_high) + (dot(factor[0], y_low) + dot(factor[1], y_high))
        cut = [slice(i * COLBLK, (i + 1) * COLBLK) for i in range(len(blocks_in))]
        return [(v[:rows, c], v[rows:, c]) for c in cut]

    def pairs(n):
        return [range(j, min(j + 2, n)) for j in range(0, n, 2)]

    def forward(s):
        factor = split(complex_form(*factors[s]))
        slot = place ^ s
        last = None
        for group in pairs(blocks - s):
            turned = []
            for j in group:
                begin = s * HALFCOL + j * COLBLK
                x = jnp.concatenate([r[slot, :, begin : begin + COLBLK] for r in (own, other)], axis=0)
                x = x.astype(jnp.float32)
                square = x * x
                seen = inside[:, begin : begin + COLBLK]
                c = jnp.where(seen, evaluate(COS_SERIES, square), 0.0)
                d = jnp.where(seen, evaluate(SIN_SERIES, square) * x, 0.0)
                if s > 0:
                    cosine[s, :, j * COLBLK : (j + 1) * COLBLK] = c
                    sine[s, :, j * COLBLK : (j + 1) * COLBLK] = d
                if s == 0:
                    cc, cs = col_cos[:, begin : begin + COLBLK], col_sin[:, begin : begin + COLBLK]
                    a = row_cos * cc - row_sin * cs
                    b = row_cos * cs + row_sin * cc
                else:
                    a, b = read(s - 1, j)
                a, b = c * a - d * b, c * b + d * a
                start = (2 * slices - s) * HALFCOL - j * COLBLK
                lo, hi = max(start, 0), min(start + broad, COLBLK)
                if lo < hi:
                    kept[s, :rows, lo - start : hi - start] = a[:, lo:hi]
                    kept[s, rows:, lo - start : hi - start] = b[:, lo:hi]
                turned.append((a, b))
            for j, v in zip(group, mix_rows(factor, turned)):
                parts = operand(*v)
                if j > 0:
                    mix_cols(s, j - 1, last, parts, forward_cols)
                last = parts
            yield

    def residual():
        last = None
        for group in pairs(blocks - slices):
            for j in group:
                a, b = read(slices - 1, j)
                cols = slice(j * COLBLK, (j + 1) * COLBLK)
                seen = [measured[k, side, :, cols] for side in range(2) for k in range(planes)]
                seen = jnp.concatenate(seen, axis=0).astype(jnp.float32)
                begin = slices * HALFCOL + j * COLBLK
                error = 2.0 * (a * a + b * b - seen)
                error = jnp.where(inside[:, begin : begin + COLBLK], error, 0.0)
                parts = operand(error * a, error * b)
                if j > 0:
                    mix_cols(slices, j - 1, last, parts, adjoint_cols)
                last = parts
            yield

    def backward(s):
        real_part, imag_part = factors[s]
        factor = split(complex_form(real_part.T, -imag_part.T))
        level = 2 * slices - 1 - s
        last = None
        for group in pairs(s + broad // COLBLK):
            for j, (a, b) in zip(group, mix_rows(factor, [read(level, j) for j in group])):
                start = s * HALFCOL - j * COLBLK
                lo, hi = max(start, 0), min(start + broad, COLBLK)
                if lo < hi:
                    y = kept[s, :, lo - start : hi - start]
                    part = PHASE_SCALE * (y[:rows] * b[:, lo:hi] - y[rows:] * a[:, lo:hi])
                    mine[place ^ s, :, lo - start : hi - start] = part[: 2 * height]
                    theirs[place ^ s, :, lo - start : hi - start] = part[half : half + 2 * height]
                if s > 0:
                    begin = 2 * (slices - s) * HALFCOL + j * COLBLK
                    c = cosine[s, :, begin : begin + COLBLK]
                    d = sine[s, :, begin : begin + COLBLK]
                    parts = operand(c * a + d * b, c * b - d * a)
                    if j > 0:
                        mix_cols(level + 1, j - 1, last, parts, adjoint_cols)
                    last = parts
            yield

    stages = [forward(s) for s in range(slices)] + [residual()] + [backward(s) for s in reversed(range(slices))]
    counts = [blocks - s for s in range(slices)] + [blocks - slices] + [s + broad // COLBLK for s in reversed(range(slices))]
    order = [(2 * k + t, k) for k, n in enumerate(counts) for t in range(len(pairs(n)))]
    for _, k in sorted(order):
        next(stages[k])


def arrange(sizes, *refs):
    slices, broad = sizes[0], sizes[4]
    place = lax.axis_index("depth")
    group = lax.axis_index("row") // 2 % 2
    out = refs[-1]
    for j in range(slices):
        for i in range(2):
            block = (group ^ i) * slices + (place ^ j)
            out[0, :, pl.ds(pl.multiple_of(block * broad, broad), broad)] = refs[j][i]


def swap(x, axis, step):
    size = lax.axis_size(axis)
    return lax.ppermute(x, axis, [(i, i ^ step) for i in range(size)])


def window_body(index_volume, angles, offsets, measured):
    slices = lax.axis_size("depth")
    planes = lax.axis_size("row") // 2
    place = lax.axis_index("depth")
    core = lax.axis_index("row") % 2
    plane = lax.axis_index("row") // 2
    group = plane % 2
    height, columns = index_volume.shape[1:]
    rows = 2 * planes * height
    half = planes * height
    span = columns // 2
    broad = span // slices
    cone = 2 * slices * HALFCOL
    blocks = (broad + 2 * cone) // COLBLK
    width = blocks * COLBLK

    mine = lax.dynamic_index_in_dim(measured, core, 0, False)
    theirs = swap(lax.dynamic_index_in_dim(measured, 1 - core, 0, False), "row", 1)
    both = jnp.pad(jnp.stack([mine, theirs]), ((0, 0), (0, 0), (cone // 2, cone // 2)))
    first_two = [lax.dynamic_slice_in_dim(both, span * (group ^ i) + broad * place, broad + cone, 2) for i in range(2)]
    weights, first_two = lax.optimization_barrier((column_parts(), first_two))

    far = [
        lax.dynamic_slice_in_dim(index_volume[0], (span - cone) * (group ^ k % 2), span + cone, 1)
        for k in range(planes)
    ]
    far = [
        far[k] if k == 0 else swap(far[k], "row", 2 * k) if k < planes - 1 else swap(index_volume[0], "row", 2 * k)
        for k in range(planes)
    ]
    far[-1] = lax.dynamic_slice_in_dim(far[-1], (span - cone) * group, span + cone, 1)
    tilts = jnp.stack([angles - TILTS // 2, jnp.mod(3 * angles, TILTS) - TILTS // 2])
    weights, tilts, first_two, far = lax.optimization_barrier(
        (column_weights(*weights), tilts, first_two, far)
    )
    far = jnp.pad(jnp.stack(far), ((0, 0), (0, 0), (cone, cone)))
    offset_tile = jnp.broadcast_to(offsets[0].astype(jnp.bfloat16), (planes, height, COLBLK))
    parts = [lax.dynamic_slice_in_dim(far, cone * group + broad * (place ^ j), width, 2) for j in range(slices)]
    own = [jnp.concatenate([part, offset_tile], axis=2) for part in parts]
    last_sent = own[1]
    own = [own[j] if j == 0 else swap(own[j], "depth", j) for j in range(slices)]
    tiles = jnp.stack([x[0, :, width:] for x in own])
    own_first = own[0][:, :, :width].reshape(1, half, width)
    own_later = jnp.stack([x[:, :, :width] for x in own[1:]]).reshape(slices - 1, half, width)
    other_first = swap(own_first, "row", 1)
    other = jnp.concatenate([other_first, swap(own_later, "row", 1)])
    own = jnp.concatenate([own_first, own_later])

    first_two = jnp.stack([first_two[0], swap(first_two[1], "row", 2)])
    first_two, _ = lax.optimization_barrier((first_two, last_sent))
    seen = [first_two] + [swap(first_two, "row", 2 * k) for k in range(2, planes, 2)]
    seen = jnp.concatenate(seen)

    sizes = (slices, planes, height, blocks, broad, columns)
    mine, theirs = pl.pallas_call(
        functools.partial(sweep, sizes),
        out_shape=[jax.ShapeDtypeStruct((slices, 2 * height, broad), jnp.float32)] * 2,
        in_specs=[pl.BlockSpec(memory_space=pltpu.VMEM)] * 7,
        out_specs=[pl.BlockSpec(memory_space=pltpu.VMEM)] * 2,
        scratch_shapes=[
            pltpu.VMEM((slices, rows, width), jnp.float32),
            pltpu.VMEM((slices, rows, width), jnp.float32),
            pltpu.VMEM((2 * slices, blocks - 1, rows, 2 * COLBLK), jnp.float32),
            pltpu.VMEM((slices, 2 * rows, broad), jnp.float32),
        ],
        compiler_params=pltpu.CompilerParams(vmem_limit_bytes=40 * 1024 * 1024),
    )(tilts, tiles, own, other, seen, *weights)

    summed = mine + swap(theirs, "row", 1)
    parts = jnp.stack([summed[:, :height], swap(summed[:, height:], "row", 2)], axis=1)
    parts = [parts[j] if j == 0 else swap(parts[j], "depth", j) for j in range(slices)]
    return pl.pallas_call(
        functools.partial(arrange, sizes),
        out_shape=jax.ShapeDtypeStruct((1, height, columns), jnp.float32),
        in_specs=[pl.BlockSpec(memory_space=pltpu.VMEM)] * slices,
        out_specs=pl.BlockSpec(memory_space=pltpu.VMEM),
        compiler_params=pltpu.CompilerParams(vmem_limit_bytes=4 * 1024 * 1024),
    )(*parts)


def suits(mesh, index_volume, measured):
    depth, row = mesh.shape["depth"], mesh.shape["row"]
    slices, rows, columns = index_volume.shape
    return (
        slices == depth
        and depth & (depth - 1) == 0
        and row & (row - 1) == 0
        and row > 2
        and measured.shape[0] == 2
        and rows == COLBLK
        and rows // row % 16 == 0
        and columns % (2 * depth * COLBLK) == 0
        and columns >= 4 * depth * HALFCOL
    )


def solution(mesh):
    in_specs = (P("depth", "row", None), P(), P("depth"), P(None, "row", None))
    out_specs = P("depth", "row", None)

    def run(index_volume, angles, offsets, measured):
        chosen = window_body if suits(mesh, index_volume, measured) else body
        mapped = jax.shard_map(chosen, mesh=mesh, in_specs=in_specs, out_specs=out_specs, check_vma=False)
        return mapped(index_volume, angles, offsets, measured)

    return run
```

```python
import functools
import math

import jax
import jax.numpy as jnp
import numpy as np
from jax import lax
from jax.experimental import pallas as pl
from jax.experimental.pallas import tpu as pltpu
from jax.sharding import PartitionSpec as P

TILTS = 16
HALF = 10
SHIFT = 4
HALFCOL = 64
COLBLK = 128


PHASE_SCALE = 0.5
CHIRP_ROW = 1.3
CHIRP_COL = 1.7


def padded_2(shard, sides, width):
    for axis, dim in sides:
        size, length = (lax.axis_size(axis), shard.shape[dim])
        up = [(i, (i + 1) % size) for i in range(size - 1)]
        down = [(j, i) for i, j in up]
        last = lax.slice_in_dim(shard, length - width, length, axis=dim)
        initial = lax.slice_in_dim(shard, 0, width, axis=dim)
        before = lax.ppermute(last, axis, up)
        after = lax.ppermute(initial, axis, down)
        shard = jnp.concatenate([before, shard, after], axis=dim)
    return shard


def from_behind(shard, axis, by):
    length = lax.axis_size(axis)
    pairs = [(i, i + by) for i in range(length) if 0 <= i + by < length]
    return lax.ppermute(shard, axis, pairs)


def kernel_values(distance, radius, chirp_rate):
    inside = jnp.abs(distance) <= radius
    phase_arg = chirp_rate / radius * distance * distance
    weight = 1.0 / math.sqrt(2 * radius + 1)
    real_part = jnp.where(inside, jnp.cos(phase_arg) * weight, 0.0)
    imag_part = jnp.where(inside, jnp.sin(phase_arg) * weight, 0.0)
    return (real_part, imag_part)


def row_band(offset, height, margin, conjugate):
    extent = (height, height + 2 * margin)
    target = lax.broadcasted_iota(jnp.int32, extent, 0)
    source = lax.broadcasted_iota(jnp.int32, extent, 1)
    offset_used = -offset if conjugate else offset
    distance = (source - target - margin - offset_used).astype(jnp.float32)
    real_part, imag_part = kernel_values(distance, HALF, CHIRP_ROW)
    return (real_part, -imag_part) if conjugate else (real_part, imag_part)


def column_band(conjugate, block_width):
    extent = (block_width + 2 * HALFCOL, block_width)
    source = lax.broadcasted_iota(jnp.int32, extent, 0)
    target = lax.broadcasted_iota(jnp.int32, extent, 1)
    distance = (source - target - HALFCOL).astype(jnp.float32)
    real_part, imag_part = kernel_values(distance, HALFCOL, CHIRP_COL)
    return (real_part, -imag_part) if conjugate else (real_part, imag_part)


def mix_rows(band, extended):

    def product(matrix, operand):
        return jnp.einsum("ij,mjc->mic", matrix, operand, precision=lax.Precision.HIGHEST)

    real_part = product(band[0], extended[:, 0]) - product(band[1], extended[:, 1])
    imag_part = product(band[0], extended[:, 1]) + product(band[1], extended[:, 0])
    return jnp.stack([real_part, imag_part], axis=1)


def block_product(window, band):

    def product(operand, matrix):
        return jnp.einsum("mrbj,ji->mrbi", operand, matrix, precision=lax.Precision.HIGHEST)

    real_part = product(window[:, 0], band[0]) - product(window[:, 1], band[1])
    imag_part = product(window[:, 1], band[0]) + product(window[:, 0], band[1])
    return jnp.stack([real_part, imag_part], axis=1)


def mix_columns(band, field):
    amount, _, height, columns = field.shape
    blocks = columns // COLBLK
    padded = jnp.pad(field, ((0, 0), (0, 0), (0, 0), (HALFCOL, COLBLK - HALFCOL)))
    middle = padded[..., :columns].reshape(amount, 2, height, blocks, COLBLK)
    beyond = padded[..., COLBLK : columns + COLBLK].reshape(amount, 2, height, blocks, COLBLK)
    window = jnp.concatenate([middle, beyond], axis=4)
    return block_product(window, band).reshape(amount, 2, height, columns)


def rotate(field, cosine, sine):
    real_part = cosine * field[:, 0] - sine * field[:, 1]
    imag_part = cosine * field[:, 1] + sine * field[:, 0]
    return jnp.stack([real_part, imag_part], axis=1)


def slab_forward(field, index_volume, offsets, active):
    margin = HALF + SHIFT
    height = field.shape[2]
    col_band = column_band(False, COLBLK)
    phase_arg = PHASE_SCALE * index_volume[0].astype(jnp.float32)
    transmitted = rotate(field, jnp.cos(phase_arg), jnp.sin(phase_arg))
    stored_fields = [transmitted]
    extended = padded_2(transmitted, (("row", 2),), margin)
    band = row_band(offsets[0], height, margin, False)

    def advance(operand, band=band):
        return mix_columns(col_band, mix_rows(band, operand))

    def remain(operand):
        return operand[:, :, margin : margin + height, :]

    field = lax.cond(active, advance, remain, extended)
    return (field, jnp.stack(stored_fields, axis=0))


def slab_adjoint(adjoint, stored, index_volume, offsets, active):
    margin = HALF + SHIFT
    height = adjoint.shape[2]
    col_band = column_band(True, COLBLK)
    layers = index_volume.shape[0]
    slab_grads = [None] * layers

    def column_step(operand):
        return mix_columns(col_band, operand)

    def unchanged(operand):
        return operand

    def remain(operand):
        return operand[:, :, margin : margin + height, :]

    for layer_no in reversed(range(layers)):
        returned = lax.cond(active, column_step, unchanged, adjoint)
        extended = padded_2(returned, (("row", 2),), margin)
        band = row_band(offsets[layer_no], height, margin, True)

        def row_step(operand, band=band):
            return mix_rows(band, operand)

        returned = lax.cond(active, row_step, remain, extended)
        transmitted = stored[layer_no]
        slab_grads[layer_no] = PHASE_SCALE * jnp.sum(
            transmitted[:, 0] * returned[:, 1] - transmitted[:, 1] * returned[:, 0], axis=0
        )
        phase_arg = PHASE_SCALE * index_volume[layer_no].astype(jnp.float32)
        adjoint = rotate(returned, jnp.cos(phase_arg), -jnp.sin(phase_arg))
    return (adjoint, jnp.stack(slab_grads, axis=0))


def plane_waves(angles, row_start, height, columns, total_rows, total_cols):
    across = angles - TILTS // 2
    along = jnp.mod(3 * angles, TILTS) - TILTS // 2
    row_index = row_start + lax.broadcasted_iota(jnp.int32, (height, columns), 0)
    col_index = lax.broadcasted_iota(jnp.int32, (height, columns), 1)
    period = total_cols * total_rows
    cycles_int = jnp.mod(
        across[:, None, None] * col_index[None] * total_rows
        + along[:, None, None] * row_index[None] * total_cols,
        period,
    )
    phase_arg = 2.0 * math.pi / period * cycles_int.astype(jnp.float32)
    return jnp.stack([jnp.cos(phase_arg), jnp.sin(phase_arg)], axis=1)


def body(index_volume, angles, offsets, measured):
    sections = lax.axis_size("depth")
    section_no = lax.axis_index("depth")
    number = angles.shape[0]
    layers = index_volume.shape[0]
    height = index_volume.shape[1]
    columns = index_volume.shape[2]
    row_start = lax.axis_index("row") * height
    total_rows = height * lax.axis_size("row")
    intensity = measured.astype(jnp.float32)
    grad_init = jnp.zeros((layers, height, columns), jnp.float32)
    incident = plane_waves(angles, row_start, height, columns, total_rows, columns)
    kept_init = jnp.zeros((layers,) + incident.shape, jnp.float32)

    def forward_compute(counter, received, stored, exit_field):
        angle_no = counter - section_no
        active = (angle_no >= 0) & (angle_no < number)
        chosen = jnp.clip(angle_no, 0, number - 1)
        entering = jnp.where(
            section_no == 0, lax.dynamic_slice_in_dim(incident, chosen, 1, 0), received
        )
        result, kept = slab_forward(entering, index_volume, offsets, active)
        placed_kept = lax.dynamic_update_slice_in_dim(stored, kept, chosen, 1)
        stored = jnp.where(active, placed_kept, stored)
        placed = lax.dynamic_update_slice_in_dim(exit_field, result, chosen, 0)
        exit_field = jnp.where(active, placed, exit_field)
        return (result, stored, exit_field)

    def forward_turn(counter, carried):
        result, stored, exit_field = forward_compute(counter, carried[0], carried[1], carried[2])
        return (from_behind(result, "depth", 1), stored, exit_field)

    zero_single = jnp.zeros((1,) + incident.shape[1:], jnp.float32)
    turns = sections + number - 1
    received, stored, exit_field = lax.fori_loop(
        0, turns - 1, forward_turn, (zero_single, kept_init, jnp.zeros_like(incident))
    )
    leftover, stored, exit_field = forward_compute(turns - 1, received, stored, exit_field)
    errors = exit_field[:, 0] * exit_field[:, 0] + exit_field[:, 1] * exit_field[:, 1] - intensity
    exit_adjoint = 2.0 * errors[:, None] * exit_field

    def backward_compute(counter, received, gradient):
        angle_no = counter - (sections - 1 - section_no)
        active = (angle_no >= 0) & (angle_no < number)
        chosen = jnp.clip(angle_no, 0, number - 1)
        entering = jnp.where(
            section_no == sections - 1,
            lax.dynamic_slice_in_dim(exit_adjoint, chosen, 1, 0),
            received,
        )
        result, slab_terms = slab_adjoint(
            entering, lax.dynamic_slice_in_dim(stored, chosen, 1, 1), index_volume, offsets, active
        )
        return (result, jnp.where(active, gradient + slab_terms, gradient))

    def backward_turn(counter, carried):
        result, gradient = backward_compute(counter, carried[0], carried[1])
        return (from_behind(result, "depth", -1), gradient)

    received, gradient = lax.fori_loop(0, turns - 1, backward_turn, (zero_single, grad_init))
    leftover, gradient = backward_compute(turns - 1, received, gradient)
    return gradient


def taps_of(radius, chirp_rate):
    distance = np.arange(-radius, radius + 1, dtype=np.float64)
    phase_arg = chirp_rate / radius * distance * distance
    weight = 1.0 / math.sqrt(2 * radius + 1)
    return (np.cos(phase_arg) * weight, np.sin(phase_arg) * weight)


def column_parts():
    taps = taps_of(HALFCOL, CHIRP_COL)
    source = np.arange(COLBLK + 2 * HALFCOL)[:, None]
    target = np.arange(COLBLK)[None, :]
    place = source - target
    inside = (place >= 0) & (place <= 2 * HALFCOL)
    parts = [np.where(inside, t[np.clip(place, 0, 2 * HALFCOL)], 0.0) for t in taps]
    high = [part.astype(jnp.bfloat16) for part in parts]
    low = [(part - h.astype(np.float64)).astype(jnp.bfloat16) for part, h in zip(parts, high)]
    return [[jnp.asarray(part) for part in pair] for pair in (high, low)]


def column_weights(high, low):
    results = []
    for sign in (1, -1):
        rows = []
        for real_part, imag_part in (high, low):
            rows.append(jnp.concatenate([real_part, sign * imag_part], axis=1))
            rows.append(jnp.concatenate([-sign * imag_part, real_part], axis=1))
        results.append(jnp.concatenate(rows))
    return results


def series(kind, degree):
    nodes = np.cos((np.arange(40) + 0.5) * np.pi / 40) * 8.0 + 8.0
    x = np.sqrt(nodes)
    values = np.cos(PHASE_SCALE * x) if kind == "cos" else np.sin(PHASE_SCALE * x) / x
    fitted = np.polynomial.chebyshev.Chebyshev.fit(nodes, values, degree, domain=[0.0, 16.0])
    return [float(v) for v in fitted.convert(kind=np.polynomial.Polynomial).coef]


COS_SERIES = series("cos", 5)
SIN_SERIES = series("sin", 5)


def evaluate(coefficients, x):
    total = x * coefficients[-1] + coefficients[-2]
    for value in coefficients[-3::-1]:
        total = total * x + value
    return total


def split(x):
    high = x.astype(jnp.bfloat16)
    return (high, (x - high.astype(jnp.float32)).astype(jnp.bfloat16))


def dot(a, b):
    return jnp.dot(a, b, preferred_element_type=jnp.float32)


def row_factor(rows_of, rows_across, offset):
    n = rows_of.shape[0]
    distance = jnp.abs(rows_across - rows_of - offset)
    cosines, sines = taps_of(HALF, CHIRP_ROW)
    real_part = jnp.zeros((n, n), jnp.float32)
    imag_part = jnp.zeros((n, n), jnp.float32)
    for k in range(HALF + 1):
        hit = distance == k
        real_part = jnp.where(hit, float(cosines[HALF + k]), real_part)
        imag_part = jnp.where(hit, float(sines[HALF + k]), imag_part)
    return (real_part, imag_part)


def complex_form(real_part, imag_part):
    upper = jnp.concatenate([real_part, -imag_part], axis=1)
    lower = jnp.concatenate([imag_part, real_part], axis=1)
    return jnp.concatenate([upper, lower], axis=0)


def sweep(sizes, tilts, tiles, own, other, measured, forward_cols, adjoint_cols, mine, theirs, cosine, sine, field, kept):
    slices, planes, height, blocks, broad, columns = sizes
    half = planes * height
    rows = 2 * half
    place = lax.axis_index("depth")
    core = lax.axis_index("row") % 2
    plane = lax.axis_index("row") // 2
    block = plane % 2 * slices + place
    across, along = [jnp.where(core == 0, tilts[i : i + 1, :1], tilts[i : i + 1, 1:]) for i in range(2)]

    def row_numbers(axis):
        i = lax.broadcasted_iota(jnp.int32, (rows, rows), axis)
        side = i // half
        step = (i - side * half) // height
        return 2 * height * (plane ^ step) + height * (core ^ side) + i % height

    rows_of, rows_across = row_numbers(0), row_numbers(1)
    walk_off = [tiles[place ^ s, :1].astype(jnp.int32) for s in range(slices)]
    factors = [row_factor(rows_of, rows_across, offset) for offset in walk_off]
    width = blocks * COLBLK
    first = block * broad - 2 * slices * HALFCOL
    lane = first + lax.broadcasted_iota(jnp.int32, (1, width), 1)
    inside = (lane >= 0) & (lane < columns)

    def wave(count, period):
        count = lax.rem(count, period)
        count = jnp.where(2 * count >= period, count - period, count)
        count = jnp.where(2 * count < -period, count + period, count)
        x = 2.0 * math.pi / period * count.astype(jnp.float32)
        c = evaluate(COS_SERIES, x * x)
        d = evaluate(SIN_SERIES, x * x) * x
        return (1.0 - 2.0 * d * d, 2.0 * c * d)

    row_cos, row_sin = wave(along * rows_of, rows)
    col_cos, col_sin = wave(across * lane, columns)

    def read(level, j):
        return (field[level, j, :, :COLBLK], field[level, j, :, COLBLK:])

    def operand(a, b):
        a_high, a_low = split(a)
        b_high, b_low = split(b)
        return (a_high, b_high, a_low, b_low)

    def mix_cols(level, j, left, right, weights):
        wide = jnp.concatenate([part for pair in zip(left, right) for part in pair], axis=1)
        high, low = wide[:, : 4 * COLBLK], wide[:, 4 * COLBLK :]
        total = dot(high, weights[: 4 * COLBLK]) + (dot(low, weights[: 4 * COLBLK]) + dot(high, weights[4 * COLBLK :]))
        field[level, j] = total

    def mix_rows(factor, blocks_in):
        y = jnp.concatenate([jnp.concatenate([a, b], axis=0) for a, b in blocks_in], axis=1)
        y_high, y_low = split(y)
        v = dot(factor[0], y_high) + (dot(factor[0], y_low) + dot(factor[1], y_high))
        cut = [slice(i * COLBLK, (i + 1) * COLBLK) for i in range(len(blocks_in))]
        return [(v[:rows, c], v[rows:, c]) for c in cut]

    def pairs(n):
        return [range(j, min(j + 2, n)) for j in range(0, n, 2)]

    low_half = lax.broadcasted_iota(jnp.int32, (rows, COLBLK), 1) < HALFCOL

    def forward(s):
        factor = split(complex_form(*factors[s]))
        slot = place ^ s

        def index_block(b):
            cols = slice(b * COLBLK, (b + 1) * COLBLK)
            x = jnp.concatenate([r[slot, :, cols] for r in (own, other)], axis=0).astype(jnp.float32)
            return pltpu.roll(x, HALFCOL, 1) if s % 2 else x

        ahead = index_block(s // 2)
        last = None
        for group in pairs(blocks - s):
            turned = []
            for j in group:
                begin = s * HALFCOL + j * COLBLK
                x = ahead
                if s % 2:
                    ahead = index_block(s // 2 + j + 1)
                    x = jnp.where(low_half, x, ahead)
                elif j + 1 < blocks - s:
                    ahead = index_block(s // 2 + j + 1)
                square = x * x
                seen = inside[:, begin : begin + COLBLK]
                c = jnp.where(seen, evaluate(COS_SERIES, square), 0.0)
                d = jnp.where(seen, evaluate(SIN_SERIES, square) * x, 0.0)
                if s > 0:
                    cosine[s, :, j * COLBLK : (j + 1) * COLBLK] = c
                    sine[s, :, j * COLBLK : (j + 1) * COLBLK] = d
                if s == 0:
                    cc, cs = col_cos[:, begin : begin + COLBLK], col_sin[:, begin : begin + COLBLK]
                    a = row_cos * cc - row_sin * cs
                    b = row_cos * cs + row_sin * cc
                else:
                    a, b = read(s - 1, j)
                a, b = c * a - d * b, c * b + d * a
                start = (2 * slices - s) * HALFCOL - j * COLBLK
                later = j - (slices - s)
                if max(start, 0) < min(start + broad, COLBLK):
                    kept[s, later, :rows] = a
                    kept[s, later, rows:] = b
                turned.append((a, b))
            for j, v in zip(group, mix_rows(factor, turned)):
                parts = operand(*v)
                if j > 0:
                    mix_cols(s, j - 1, last, parts, forward_cols)
                last = parts
            yield

    def residual():
        last = None
        for group in pairs(blocks - slices):
            for j in group:
                a, b = read(slices - 1, j)
                cols = slice(j * COLBLK, (j + 1) * COLBLK)
                seen = [measured[k, side, :, cols] for side in range(2) for k in range(planes)]
                seen = jnp.concatenate(seen, axis=0).astype(jnp.float32)
                begin = slices * HALFCOL + j * COLBLK
                error = 2.0 * (a * a + b * b - seen)
                error = jnp.where(inside[:, begin : begin + COLBLK], error, 0.0)
                parts = operand(error * a, error * b)
                if j > 0:
                    mix_cols(slices, j - 1, last, parts, adjoint_cols)
                last = parts
            yield

    def backward(s):
        real_part, imag_part = factors[s]
        factor = split(complex_form(real_part.T, -imag_part.T))
        level = 2 * slices - 1 - s
        last = None
        for group in pairs(s + broad // COLBLK):
            for j, (a, b) in zip(group, mix_rows(factor, [read(level, j) for j in group])):
                start = s * HALFCOL - j * COLBLK
                lo, hi = max(start, 0), min(start + broad, COLBLK)
                if lo < hi:
                    part = PHASE_SCALE * (kept[s, j, :rows] * b - kept[s, j, rows:] * a)[:, lo:hi]
                    mine[place ^ s, :, lo - start : hi - start] = part[: 2 * height]
                    theirs[place ^ s, :, lo - start : hi - start] = part[half : half + 2 * height]
                if s > 0:
                    begin = 2 * (slices - s) * HALFCOL + j * COLBLK
                    c = cosine[s, :, begin : begin + COLBLK]
                    d = sine[s, :, begin : begin + COLBLK]
                    parts = operand(c * a + d * b, c * b - d * a)
                    if j > 0:
                        mix_cols(level + 1, j - 1, last, parts, adjoint_cols)
                    last = parts
            yield

    stages = [forward(s) for s in range(slices)] + [residual()] + [backward(s) for s in reversed(range(slices))]
    counts = [blocks - s for s in range(slices)] + [blocks - slices] + [s + broad // COLBLK for s in reversed(range(slices))]
    order = [(2 * k + t, k) for k, n in enumerate(counts) for t in range(len(pairs(n)))]
    for _, k in sorted(order):
        next(stages[k])


def arrange(sizes, *refs):
    slices, broad = sizes[0], sizes[4]
    place = lax.axis_index("depth")
    group = lax.axis_index("row") // 2 % 2
    out = refs[-1]
    for j in range(slices):
        for i in range(2):
            block = (group ^ i) * slices + (place ^ j)
            out[0, :, pl.ds(pl.multiple_of(block * broad, broad), broad)] = refs[j][i]


def swap(x, axis, step):
    size = lax.axis_size(axis)
    return lax.ppermute(x, axis, [(i, i ^ step) for i in range(size)])


def window_body(index_volume, angles, offsets, measured):
    slices = lax.axis_size("depth")
    planes = lax.axis_size("row") // 2
    place = lax.axis_index("depth")
    core = lax.axis_index("row") % 2
    plane = lax.axis_index("row") // 2
    group = plane % 2
    height, columns = index_volume.shape[1:]
    rows = 2 * planes * height
    half = planes * height
    span = columns // 2
    broad = span // slices
    cone = 2 * slices * HALFCOL
    blocks = (broad + 2 * cone) // COLBLK
    width = blocks * COLBLK

    mine = lax.dynamic_index_in_dim(measured, core, 0, False)
    theirs = swap(lax.dynamic_index_in_dim(measured, 1 - core, 0, False), "row", 1)
    both = jnp.pad(jnp.stack([mine, theirs]), ((0, 0), (0, 0), (cone // 2, cone // 2)))
    first_two = [lax.dynamic_slice_in_dim(both, span * (group ^ i) + broad * place, broad + cone, 2) for i in range(2)]
    weights, first_two = lax.optimization_barrier((column_parts(), first_two))

    far = [
        lax.dynamic_slice_in_dim(index_volume[0], (span - cone) * (group ^ k % 2), span + cone, 1)
        for k in range(planes)
    ]
    far = [
        far[k] if k == 0 else swap(far[k], "row", 2 * k) if k < planes - 1 else swap(index_volume[0], "row", 2 * k)
        for k in range(planes)
    ]
    far[-1] = lax.dynamic_slice_in_dim(far[-1], (span - cone) * group, span + cone, 1)
    tilts = jnp.stack([angles - TILTS // 2, jnp.mod(3 * angles, TILTS) - TILTS // 2])
    weights, tilts, first_two, far = lax.optimization_barrier(
        (column_weights(*weights), tilts, first_two, far)
    )
    far = jnp.pad(jnp.stack(far), ((0, 0), (0, 0), (cone, cone)))
    offset_tile = jnp.broadcast_to(offsets[0].astype(jnp.bfloat16), (planes, height, COLBLK))
    parts = [lax.dynamic_slice_in_dim(far, cone * group + broad * (place ^ j), width, 2) for j in range(slices)]
    own = [jnp.concatenate([part, offset_tile], axis=2) for part in parts]
    last_sent = own[1]
    own = [own[j] if j == 0 else swap(own[j], "depth", j) for j in range(slices)]
    tiles = jnp.stack([x[0, :, width:] for x in own])
    own_first = own[0][:, :, :width].reshape(1, half, width)
    own_later = jnp.stack([x[:, :, :width] for x in own[1:]]).reshape(slices - 1, half, width)
    other_first = swap(own_first, "row", 1)
    other = jnp.concatenate([other_first, swap(own_later, "row", 1)])
    own = jnp.concatenate([own_first, own_later])

    first_two = jnp.stack([first_two[0], swap(first_two[1], "row", 2)])
    first_two, _ = lax.optimization_barrier((first_two, last_sent))
    seen = [first_two] + [swap(first_two, "row", 2 * k) for k in range(2, planes, 2)]
    seen = jnp.concatenate(seen)

    sizes = (slices, planes, height, blocks, broad, columns)
    mine, theirs = pl.pallas_call(
        functools.partial(sweep, sizes),
        out_shape=[jax.ShapeDtypeStruct((slices, 2 * height, broad), jnp.float32)] * 2,
        in_specs=[pl.BlockSpec(memory_space=pltpu.VMEM)] * 7,
        out_specs=[pl.BlockSpec(memory_space=pltpu.VMEM)] * 2,
        scratch_shapes=[
            pltpu.VMEM((slices, rows, width), jnp.float32),
            pltpu.VMEM((slices, rows, width), jnp.float32),
            pltpu.VMEM((2 * slices, blocks - 1, rows, 2 * COLBLK), jnp.float32),
            pltpu.VMEM((slices, slices - 1 + broad // COLBLK, 2 * rows, COLBLK), jnp.float32),
        ],
        compiler_params=pltpu.CompilerParams(vmem_limit_bytes=40 * 1024 * 1024),
    )(tilts, tiles, own, other, seen, *weights)

    summed = mine + swap(theirs, "row", 1)
    parts = jnp.stack([summed[:, :height], swap(summed[:, height:], "row", 2)], axis=1)
    parts = [parts[j] if j == 0 else swap(parts[j], "depth", j) for j in range(slices)]
    return pl.pallas_call(
        functools.partial(arrange, sizes),
        out_shape=jax.ShapeDtypeStruct((1, height, columns), jnp.float32),
        in_specs=[pl.BlockSpec(memory_space=pltpu.VMEM)] * slices,
        out_specs=pl.BlockSpec(memory_space=pltpu.VMEM),
        compiler_params=pltpu.CompilerParams(vmem_limit_bytes=4 * 1024 * 1024),
    )(*parts)


def suits(mesh, index_volume, measured):
    depth, row = mesh.shape["depth"], mesh.shape["row"]
    slices, rows, columns = index_volume.shape
    return (
        slices == depth
        and depth & (depth - 1) == 0
        and row & (row - 1) == 0
        and row > 2
        and measured.shape[0] == 2
        and rows == COLBLK
        and rows // row % 16 == 0
        and columns % (2 * depth * COLBLK) == 0
        and columns >= 4 * depth * HALFCOL
    )


def solution(mesh):
    in_specs = (P("depth", "row", None), P(), P("depth"), P(None, "row", None))
    out_specs = P("depth", "row", None)

    def run(index_volume, angles, offsets, measured):
        chosen = window_body if suits(mesh, index_volume, measured) else body
        mapped = jax.shard_map(chosen, mesh=mesh, in_specs=in_specs, out_specs=out_specs, check_vma=False)
        return mapped(index_volume, angles, offsets, measured)

    return run
```

```python
import functools
import math

import jax
import jax.numpy as jnp
import numpy as np
from jax import lax
from jax.experimental import pallas as pl
from jax.experimental.pallas import tpu as pltpu
from jax.sharding import PartitionSpec as P

TILTS = 16
HALF = 10
SHIFT = 4
HALFCOL = 64
COLBLK = 128


PHASE_SCALE = 0.5
CHIRP_ROW = 1.3
CHIRP_COL = 1.7


def padded_2(shard, sides, width):
    for axis, dim in sides:
        size, length = (lax.axis_size(axis), shard.shape[dim])
        up = [(i, (i + 1) % size) for i in range(size - 1)]
        down = [(j, i) for i, j in up]
        last = lax.slice_in_dim(shard, length - width, length, axis=dim)
        initial = lax.slice_in_dim(shard, 0, width, axis=dim)
        before = lax.ppermute(last, axis, up)
        after = lax.ppermute(initial, axis, down)
        shard = jnp.concatenate([before, shard, after], axis=dim)
    return shard


def from_behind(shard, axis, by):
    length = lax.axis_size(axis)
    pairs = [(i, i + by) for i in range(length) if 0 <= i + by < length]
    return lax.ppermute(shard, axis, pairs)


def kernel_values(distance, radius, chirp_rate):
    inside = jnp.abs(distance) <= radius
    phase_arg = chirp_rate / radius * distance * distance
    weight = 1.0 / math.sqrt(2 * radius + 1)
    real_part = jnp.where(inside, jnp.cos(phase_arg) * weight, 0.0)
    imag_part = jnp.where(inside, jnp.sin(phase_arg) * weight, 0.0)
    return (real_part, imag_part)


def row_band(offset, height, margin, conjugate):
    extent = (height, height + 2 * margin)
    target = lax.broadcasted_iota(jnp.int32, extent, 0)
    source = lax.broadcasted_iota(jnp.int32, extent, 1)
    offset_used = -offset if conjugate else offset
    distance = (source - target - margin - offset_used).astype(jnp.float32)
    real_part, imag_part = kernel_values(distance, HALF, CHIRP_ROW)
    return (real_part, -imag_part) if conjugate else (real_part, imag_part)


def column_band(conjugate, block_width):
    extent = (block_width + 2 * HALFCOL, block_width)
    source = lax.broadcasted_iota(jnp.int32, extent, 0)
    target = lax.broadcasted_iota(jnp.int32, extent, 1)
    distance = (source - target - HALFCOL).astype(jnp.float32)
    real_part, imag_part = kernel_values(distance, HALFCOL, CHIRP_COL)
    return (real_part, -imag_part) if conjugate else (real_part, imag_part)


def mix_rows(band, extended):

    def product(matrix, operand):
        return jnp.einsum("ij,mjc->mic", matrix, operand, precision=lax.Precision.HIGHEST)

    real_part = product(band[0], extended[:, 0]) - product(band[1], extended[:, 1])
    imag_part = product(band[0], extended[:, 1]) + product(band[1], extended[:, 0])
    return jnp.stack([real_part, imag_part], axis=1)


def block_product(window, band):

    def product(operand, matrix):
        return jnp.einsum("mrbj,ji->mrbi", operand, matrix, precision=lax.Precision.HIGHEST)

    real_part = product(window[:, 0], band[0]) - product(window[:, 1], band[1])
    imag_part = product(window[:, 1], band[0]) + product(window[:, 0], band[1])
    return jnp.stack([real_part, imag_part], axis=1)


def mix_columns(band, field):
    amount, _, height, columns = field.shape
    blocks = columns // COLBLK
    padded = jnp.pad(field, ((0, 0), (0, 0), (0, 0), (HALFCOL, COLBLK - HALFCOL)))
    middle = padded[..., :columns].reshape(amount, 2, height, blocks, COLBLK)
    beyond = padded[..., COLBLK : columns + COLBLK].reshape(amount, 2, height, blocks, COLBLK)
    window = jnp.concatenate([middle, beyond], axis=4)
    return block_product(window, band).reshape(amount, 2, height, columns)


def rotate(field, cosine, sine):
    real_part = cosine * field[:, 0] - sine * field[:, 1]
    imag_part = cosine * field[:, 1] + sine * field[:, 0]
    return jnp.stack([real_part, imag_part], axis=1)


def slab_forward(field, index_volume, offsets, active):
    margin = HALF + SHIFT
    height = field.shape[2]
    col_band = column_band(False, COLBLK)
    phase_arg = PHASE_SCALE * index_volume[0].astype(jnp.float32)
    transmitted = rotate(field, jnp.cos(phase_arg), jnp.sin(phase_arg))
    stored_fields = [transmitted]
    extended = padded_2(transmitted, (("row", 2),), margin)
    band = row_band(offsets[0], height, margin, False)

    def advance(operand, band=band):
        return mix_columns(col_band, mix_rows(band, operand))

    def remain(operand):
        return operand[:, :, margin : margin + height, :]

    field = lax.cond(active, advance, remain, extended)
    return (field, jnp.stack(stored_fields, axis=0))


def slab_adjoint(adjoint, stored, index_volume, offsets, active):
    margin = HALF + SHIFT
    height = adjoint.shape[2]
    col_band = column_band(True, COLBLK)
    layers = index_volume.shape[0]
    slab_grads = [None] * layers

    def column_step(operand):
        return mix_columns(col_band, operand)

    def unchanged(operand):
        return operand

    def remain(operand):
        return operand[:, :, margin : margin + height, :]

    for layer_no in reversed(range(layers)):
        returned = lax.cond(active, column_step, unchanged, adjoint)
        extended = padded_2(returned, (("row", 2),), margin)
        band = row_band(offsets[layer_no], height, margin, True)

        def row_step(operand, band=band):
            return mix_rows(band, operand)

        returned = lax.cond(active, row_step, remain, extended)
        transmitted = stored[layer_no]
        slab_grads[layer_no] = PHASE_SCALE * jnp.sum(
            transmitted[:, 0] * returned[:, 1] - transmitted[:, 1] * returned[:, 0], axis=0
        )
        phase_arg = PHASE_SCALE * index_volume[layer_no].astype(jnp.float32)
        adjoint = rotate(returned, jnp.cos(phase_arg), -jnp.sin(phase_arg))
    return (adjoint, jnp.stack(slab_grads, axis=0))


def plane_waves(angles, row_start, height, columns, total_rows, total_cols):
    across = angles - TILTS // 2
    along = jnp.mod(3 * angles, TILTS) - TILTS // 2
    row_index = row_start + lax.broadcasted_iota(jnp.int32, (height, columns), 0)
    col_index = lax.broadcasted_iota(jnp.int32, (height, columns), 1)
    period = total_cols * total_rows
    cycles_int = jnp.mod(
        across[:, None, None] * col_index[None] * total_rows
        + along[:, None, None] * row_index[None] * total_cols,
        period,
    )
    phase_arg = 2.0 * math.pi / period * cycles_int.astype(jnp.float32)
    return jnp.stack([jnp.cos(phase_arg), jnp.sin(phase_arg)], axis=1)


def body(index_volume, angles, offsets, measured):
    sections = lax.axis_size("depth")
    section_no = lax.axis_index("depth")
    number = angles.shape[0]
    layers = index_volume.shape[0]
    height = index_volume.shape[1]
    columns = index_volume.shape[2]
    row_start = lax.axis_index("row") * height
    total_rows = height * lax.axis_size("row")
    intensity = measured.astype(jnp.float32)
    grad_init = jnp.zeros((layers, height, columns), jnp.float32)
    incident = plane_waves(angles, row_start, height, columns, total_rows, columns)
    kept_init = jnp.zeros((layers,) + incident.shape, jnp.float32)

    def forward_compute(counter, received, stored, exit_field):
        angle_no = counter - section_no
        active = (angle_no >= 0) & (angle_no < number)
        chosen = jnp.clip(angle_no, 0, number - 1)
        entering = jnp.where(
            section_no == 0, lax.dynamic_slice_in_dim(incident, chosen, 1, 0), received
        )
        result, kept = slab_forward(entering, index_volume, offsets, active)
        placed_kept = lax.dynamic_update_slice_in_dim(stored, kept, chosen, 1)
        stored = jnp.where(active, placed_kept, stored)
        placed = lax.dynamic_update_slice_in_dim(exit_field, result, chosen, 0)
        exit_field = jnp.where(active, placed, exit_field)
        return (result, stored, exit_field)

    def forward_turn(counter, carried):
        result, stored, exit_field = forward_compute(counter, carried[0], carried[1], carried[2])
        return (from_behind(result, "depth", 1), stored, exit_field)

    zero_single = jnp.zeros((1,) + incident.shape[1:], jnp.float32)
    turns = sections + number - 1
    received, stored, exit_field = lax.fori_loop(
        0, turns - 1, forward_turn, (zero_single, kept_init, jnp.zeros_like(incident))
    )
    leftover, stored, exit_field = forward_compute(turns - 1, received, stored, exit_field)
    errors = exit_field[:, 0] * exit_field[:, 0] + exit_field[:, 1] * exit_field[:, 1] - intensity
    exit_adjoint = 2.0 * errors[:, None] * exit_field

    def backward_compute(counter, received, gradient):
        angle_no = counter - (sections - 1 - section_no)
        active = (angle_no >= 0) & (angle_no < number)
        chosen = jnp.clip(angle_no, 0, number - 1)
        entering = jnp.where(
            section_no == sections - 1,
            lax.dynamic_slice_in_dim(exit_adjoint, chosen, 1, 0),
            received,
        )
        result, slab_terms = slab_adjoint(
            entering, lax.dynamic_slice_in_dim(stored, chosen, 1, 1), index_volume, offsets, active
        )
        return (result, jnp.where(active, gradient + slab_terms, gradient))

    def backward_turn(counter, carried):
        result, gradient = backward_compute(counter, carried[0], carried[1])
        return (from_behind(result, "depth", -1), gradient)

    received, gradient = lax.fori_loop(0, turns - 1, backward_turn, (zero_single, grad_init))
    leftover, gradient = backward_compute(turns - 1, received, gradient)
    return gradient


def taps_of(radius, chirp_rate):
    distance = np.arange(-radius, radius + 1, dtype=np.float64)
    phase_arg = chirp_rate / radius * distance * distance
    weight = 1.0 / math.sqrt(2 * radius + 1)
    return (np.cos(phase_arg) * weight, np.sin(phase_arg) * weight)


def column_parts():
    taps = taps_of(HALFCOL, CHIRP_COL)
    source = np.arange(COLBLK + 2 * HALFCOL)[:, None]
    target = np.arange(COLBLK)[None, :]
    place = source - target
    inside = (place >= 0) & (place <= 2 * HALFCOL)
    parts = [np.where(inside, t[np.clip(place, 0, 2 * HALFCOL)], 0.0) for t in taps]
    high = [part.astype(jnp.bfloat16) for part in parts]
    low = [(part - h.astype(np.float64)).astype(jnp.bfloat16) for part, h in zip(parts, high)]
    return [[jnp.asarray(part) for part in pair] for pair in (high, low)]


def column_weights(high, low):
    results = []
    for sign in (1, -1):
        rows = []
        for real_part, imag_part in (high, low):
            rows.append(jnp.concatenate([real_part, sign * imag_part], axis=1))
            rows.append(jnp.concatenate([-sign * imag_part, real_part], axis=1))
        results.append(jnp.concatenate(rows))
    return results


def series(kind, degree):
    nodes = np.cos((np.arange(40) + 0.5) * np.pi / 40) * 8.0 + 8.0
    x = np.sqrt(nodes)
    values = np.cos(PHASE_SCALE * x) if kind == "cos" else np.sin(PHASE_SCALE * x) / x
    fitted = np.polynomial.chebyshev.Chebyshev.fit(nodes, values, degree, domain=[0.0, 16.0])
    return [float(v) for v in fitted.convert(kind=np.polynomial.Polynomial).coef]


COS_SERIES = series("cos", 5)
SIN_SERIES = series("sin", 5)


def evaluate(coefficients, x):
    total = x * coefficients[-1] + coefficients[-2]
    for value in coefficients[-3::-1]:
        total = total * x + value
    return total


def split(x):
    high = x.astype(jnp.bfloat16)
    return (high, (x - high.astype(jnp.float32)).astype(jnp.bfloat16))


def dot(a, b):
    return jnp.dot(a, b, preferred_element_type=jnp.float32)


def row_factor(rows_of, rows_across, offset):
    n = rows_of.shape[0]
    distance = jnp.abs(rows_across - rows_of - offset)
    cosines, sines = taps_of(HALF, CHIRP_ROW)
    real_part = jnp.zeros((n, n), jnp.float32)
    imag_part = jnp.zeros((n, n), jnp.float32)
    for k in range(HALF + 1):
        hit = distance == k
        real_part = jnp.where(hit, float(cosines[HALF + k]), real_part)
        imag_part = jnp.where(hit, float(sines[HALF + k]), imag_part)
    return (real_part, imag_part)


def complex_form(real_part, imag_part):
    upper = jnp.concatenate([real_part, -imag_part], axis=1)
    lower = jnp.concatenate([imag_part, real_part], axis=1)
    return jnp.concatenate([upper, lower], axis=0)


def sweep(sizes, tilts, tiles, own, other, measured, forward_cols, adjoint_cols, mine, theirs, cosine, sine, field, kept):
    slices, planes, height, blocks, broad, columns = sizes
    half = planes * height
    rows = 2 * half
    place = lax.axis_index("depth")
    core = lax.axis_index("row") % 2
    plane = lax.axis_index("row") // 2
    block = plane % 2 * slices + place
    across, along = [jnp.where(core == 0, tilts[i : i + 1, :1], tilts[i : i + 1, 1:]) for i in range(2)]

    def row_numbers(axis):
        i = lax.broadcasted_iota(jnp.int32, (rows, rows), axis)
        side = i // half
        step = (i - side * half) // height
        return 2 * height * (plane ^ step) + height * (core ^ side) + i % height

    rows_of, rows_across = row_numbers(0), row_numbers(1)
    walk_off = [tiles[place ^ s, :1].astype(jnp.int32) for s in range(slices)]
    factors = [[split(part) for part in row_factor(rows_of, rows_across, offset)] for offset in walk_off]
    width = blocks * COLBLK
    first = block * broad - 2 * slices * HALFCOL
    lane = first + lax.broadcasted_iota(jnp.int32, (1, width), 1)
    inside = (lane >= 0) & (lane < columns)

    def wave(count, period):
        count = lax.rem(count, period)
        count = jnp.where(2 * count >= period, count - period, count)
        count = jnp.where(2 * count < -period, count + period, count)
        x = 2.0 * math.pi / period * count.astype(jnp.float32)
        c = evaluate(COS_SERIES, x * x)
        d = evaluate(SIN_SERIES, x * x) * x
        return (1.0 - 2.0 * d * d, 2.0 * c * d)

    row_cos, row_sin = wave(along * rows_of, rows)
    col_cos, col_sin = wave(across * lane, columns)

    def read(level, j):
        return (field[level, j, :, :COLBLK], field[level, j, :, COLBLK:])

    def operand(a, b):
        a_high, a_low = split(a)
        b_high, b_low = split(b)
        return (a_high, b_high, a_low, b_low)

    def mix_cols(level, j, left, right, weights):
        wide = jnp.concatenate([part for pair in zip(left, right) for part in pair], axis=1)
        high, low = wide[:, : 4 * COLBLK], wide[:, 4 * COLBLK :]
        total = dot(high, weights[: 4 * COLBLK]) + (dot(low, weights[: 4 * COLBLK]) + dot(high, weights[4 * COLBLK :]))
        field[level, j] = total

    def mix_rows(factor, blocks_in):
        y = jnp.concatenate([jnp.concatenate([a, b], axis=0) for a, b in blocks_in], axis=1)
        y_high, y_low = split(y)
        v = dot(factor[0], y_high) + (dot(factor[0], y_low) + dot(factor[1], y_high))
        cut = [slice(i * COLBLK, (i + 1) * COLBLK) for i in range(len(blocks_in))]
        middle = v.shape[0] // 2
        return [(v[:middle, c], v[middle:, c]) for c in cut]

    def pairs(n):
        return [range(j, min(j + 2, n)) for j in range(0, n, 2)]

    low_half = lax.broadcasted_iota(jnp.int32, (rows, COLBLK), 1) < HALFCOL

    def forward(s):
        factor = [complex_form(real_part, imag_part) for real_part, imag_part in zip(*factors[s])]
        slot = place ^ s

        def index_block(b):
            cols = slice(b * COLBLK, (b + 1) * COLBLK)
            x = jnp.concatenate([r[slot, :, cols] for r in (own, other)], axis=0).astype(jnp.float32)
            return pltpu.roll(x, HALFCOL, 1) if s % 2 else x

        ahead = index_block(s // 2)
        last = None
        for group in pairs(blocks - s):
            turned = []
            for j in group:
                begin = s * HALFCOL + j * COLBLK
                x = ahead
                if s % 2:
                    ahead = index_block(s // 2 + j + 1)
                    x = jnp.where(low_half, x, ahead)
                elif j + 1 < blocks - s:
                    ahead = index_block(s // 2 + j + 1)
                square = x * x
                seen = inside[:, begin : begin + COLBLK]
                c = jnp.where(seen, evaluate(COS_SERIES, square), 0.0)
                d = jnp.where(seen, evaluate(SIN_SERIES, square) * x, 0.0)
                if s > 0:
                    cosine[s, :, j * COLBLK : (j + 1) * COLBLK] = c
                    sine[s, :, j * COLBLK : (j + 1) * COLBLK] = d
                if s == 0:
                    cc, cs = col_cos[:, begin : begin + COLBLK], col_sin[:, begin : begin + COLBLK]
                    a = row_cos * cc - row_sin * cs
                    b = row_cos * cs + row_sin * cc
                else:
                    a, b = read(s - 1, j)
                a, b = c * a - d * b, c * b + d * a
                start = (2 * slices - s) * HALFCOL - j * COLBLK
                later = j - (slices - s)
                if max(start, 0) < min(start + broad, COLBLK):
                    kept[s, later, :rows] = a
                    kept[s, later, rows:] = b
                turned.append((a, b))
            for j, v in zip(group, mix_rows(factor, turned)):
                parts = operand(*v)
                if j > 0:
                    mix_cols(s, j - 1, last, parts, forward_cols)
                last = parts
            yield

    def residual():
        last = None
        for group in pairs(blocks - slices):
            for j in group:
                a, b = read(slices - 1, j)
                cols = slice(j * COLBLK, (j + 1) * COLBLK)
                seen = [measured[k, side, :, cols] for side in range(2) for k in range(planes)]
                seen = jnp.concatenate(seen, axis=0).astype(jnp.float32)
                begin = slices * HALFCOL + j * COLBLK
                error = 2.0 * (a * a + b * b - seen)
                error = jnp.where(inside[:, begin : begin + COLBLK], error, 0.0)
                parts = operand(error * a, error * b)
                if j > 0:
                    mix_cols(slices, j - 1, last, parts, adjoint_cols)
                last = parts
            yield

    def backward(s):
        factor = [complex_form(real_part.T, -imag_part.T) for real_part, imag_part in zip(*factors[s])]
        if s == 0:
            factor = [
                jnp.concatenate([x[i * half : i * half + 2 * height] for i in range(4)], axis=0) for x in factor
            ]
        level = 2 * slices - 1 - s
        last = None
        for group in pairs(s + broad // COLBLK):
            for j, (a, b) in zip(group, mix_rows(factor, [read(level, j) for j in group])):
                start = s * HALFCOL - j * COLBLK
                lo, hi = max(start, 0), min(start + broad, COLBLK)
                if lo < hi:
                    for i, target in enumerate((mine, theirs)):
                        held = slice(i * half, i * half + 2 * height)
                        there = slice(rows + i * half, rows + i * half + 2 * height)
                        new = slice(i * 2 * height, (i + 1) * 2 * height) if s == 0 else held
                        part = PHASE_SCALE * (kept[s, j, held] * b[new] - kept[s, j, there] * a[new])
                        target[place ^ s, :, lo - start : hi - start] = part[:, lo:hi]
                if s > 0:
                    begin = 2 * (slices - s) * HALFCOL + j * COLBLK
                    c = cosine[s, :, begin : begin + COLBLK]
                    d = sine[s, :, begin : begin + COLBLK]
                    parts = operand(c * a + d * b, c * b - d * a)
                    if j > 0:
                        mix_cols(level + 1, j - 1, last, parts, adjoint_cols)
                    last = parts
            yield

    stages = [forward(s) for s in range(slices)] + [residual()] + [backward(s) for s in reversed(range(slices))]
    counts = [blocks - s for s in range(slices)] + [blocks - slices] + [s + broad // COLBLK for s in reversed(range(slices))]
    order = [(2 * k + t, k) for k, n in enumerate(counts) for t in range(len(pairs(n)))]
    for _, k in sorted(order):
        next(stages[k])


def arrange(sizes, *refs):
    slices, broad = sizes[0], sizes[4]
    place = lax.axis_index("depth")
    group = lax.axis_index("row") // 2 % 2
    out = refs[-1]
    for j in range(slices):
        for i in range(2):
            block = (group ^ i) * slices + (place ^ j)
            out[0, :, pl.ds(pl.multiple_of(block * broad, broad), broad)] = refs[j][i]


def swap(x, axis, step):
    size = lax.axis_size(axis)
    return lax.ppermute(x, axis, [(i, i ^ step) for i in range(size)])


def window_body(index_volume, angles, offsets, measured):
    slices = lax.axis_size("depth")
    planes = lax.axis_size("row") // 2
    place = lax.axis_index("depth")
    core = lax.axis_index("row") % 2
    plane = lax.axis_index("row") // 2
    group = plane % 2
    height, columns = index_volume.shape[1:]
    rows = 2 * planes * height
    half = planes * height
    span = columns // 2
    broad = span // slices
    cone = 2 * slices * HALFCOL
    blocks = (broad + 2 * cone) // COLBLK
    width = blocks * COLBLK

    mine = lax.dynamic_index_in_dim(measured, core, 0, False)
    theirs = swap(lax.dynamic_index_in_dim(measured, 1 - core, 0, False), "row", 1)
    both = jnp.pad(jnp.stack([mine, theirs]), ((0, 0), (0, 0), (cone // 2, cone // 2)))
    first_two = [lax.dynamic_slice_in_dim(both, span * (group ^ i) + broad * place, broad + cone, 2) for i in range(2)]
    weights, first_two = lax.optimization_barrier((column_parts(), first_two))

    far = [
        lax.dynamic_slice_in_dim(index_volume[0], (span - cone) * (group ^ k % 2), span + cone, 1)
        for k in range(planes)
    ]
    far = [
        far[k] if k == 0 else swap(far[k], "row", 2 * k) if k < planes - 1 else swap(index_volume[0], "row", 2 * k)
        for k in range(planes)
    ]
    far[-1] = lax.dynamic_slice_in_dim(far[-1], (span - cone) * group, span + cone, 1)
    tilts = jnp.stack([angles - TILTS // 2, jnp.mod(3 * angles, TILTS) - TILTS // 2])
    weights, tilts, first_two, far = lax.optimization_barrier(
        (column_weights(*weights), tilts, first_two, far)
    )
    far = jnp.pad(jnp.stack(far), ((0, 0), (0, 0), (cone, cone)))
    offset_tile = jnp.broadcast_to(offsets[0].astype(jnp.bfloat16), (planes, height, COLBLK))
    parts = [lax.dynamic_slice_in_dim(far, cone * group + broad * (place ^ j), width, 2) for j in range(slices)]
    own = [jnp.concatenate([part, offset_tile], axis=2) for part in parts]
    last_sent = own[1]
    own = [own[j] if j == 0 else swap(own[j], "depth", j) for j in range(slices)]
    tiles = jnp.stack([x[0, :, width:] for x in own])
    own_first = own[0][:, :, :width].reshape(1, half, width)
    own_later = jnp.stack([x[:, :, :width] for x in own[1:]]).reshape(slices - 1, half, width)
    other_first = swap(own_first, "row", 1)
    other = jnp.concatenate([other_first, swap(own_later, "row", 1)])
    own = jnp.concatenate([own_first, own_later])

    first_two = jnp.stack([first_two[0], swap(first_two[1], "row", 2)])
    first_two, _ = lax.optimization_barrier((first_two, last_sent))
    seen = [first_two] + [swap(first_two, "row", 2 * k) for k in range(2, planes, 2)]
    seen = jnp.concatenate(seen)

    sizes = (slices, planes, height, blocks, broad, columns)
    mine, theirs = pl.pallas_call(
        functools.partial(sweep, sizes),
        out_shape=[jax.ShapeDtypeStruct((slices, 2 * height, broad), jnp.float32)] * 2,
        in_specs=[pl.BlockSpec(memory_space=pltpu.VMEM)] * 7,
        out_specs=[pl.BlockSpec(memory_space=pltpu.VMEM)] * 2,
        scratch_shapes=[
            pltpu.VMEM((slices, rows, width), jnp.float32),
            pltpu.VMEM((slices, rows, width), jnp.float32),
            pltpu.VMEM((2 * slices, blocks - 1, rows, 2 * COLBLK), jnp.float32),
            pltpu.VMEM((slices, slices - 1 + broad // COLBLK, 2 * rows, COLBLK), jnp.float32),
        ],
        compiler_params=pltpu.CompilerParams(vmem_limit_bytes=40 * 1024 * 1024),
    )(tilts, tiles, own, other, seen, *weights)

    summed = mine + swap(theirs, "row", 1)
    parts = jnp.stack([summed[:, :height], swap(summed[:, height:], "row", 2)], axis=1)
    parts = [parts[j] if j == 0 else swap(parts[j], "depth", j) for j in range(slices)]
    return pl.pallas_call(
        functools.partial(arrange, sizes),
        out_shape=jax.ShapeDtypeStruct((1, height, columns), jnp.float32),
        in_specs=[pl.BlockSpec(memory_space=pltpu.VMEM)] * slices,
        out_specs=pl.BlockSpec(memory_space=pltpu.VMEM),
        compiler_params=pltpu.CompilerParams(vmem_limit_bytes=4 * 1024 * 1024),
    )(*parts)


def suits(mesh, index_volume, measured):
    depth, row = mesh.shape["depth"], mesh.shape["row"]
    slices, rows, columns = index_volume.shape
    return (
        slices == depth
        and depth & (depth - 1) == 0
        and row & (row - 1) == 0
        and row > 2
        and measured.shape[0] == 2
        and rows == COLBLK
        and rows // row % 16 == 0
        and columns % (2 * depth * COLBLK) == 0
        and columns >= 4 * depth * HALFCOL
    )


def solution(mesh):
    in_specs = (P("depth", "row", None), P(), P("depth"), P(None, "row", None))
    out_specs = P("depth", "row", None)

    def run(index_volume, angles, offsets, measured):
        chosen = window_body if suits(mesh, index_volume, measured) else body
        mapped = jax.shard_map(chosen, mesh=mesh, in_specs=in_specs, out_specs=out_specs, check_vma=False)
        return mapped(index_volume, angles, offsets, measured)

    return run
```

```python
import functools
import math

import jax
import jax.numpy as jnp
import numpy as np
from jax import lax
from jax.experimental import pallas as pl
from jax.experimental.pallas import tpu as pltpu
from jax.sharding import PartitionSpec as P

TILTS = 16
HALF = 10
SHIFT = 4
HALFCOL = 64
COLBLK = 128


PHASE_SCALE = 0.5
CHIRP_ROW = 1.3
CHIRP_COL = 1.7


def padded_2(shard, sides, width):
    for axis, dim in sides:
        size, length = (lax.axis_size(axis), shard.shape[dim])
        up = [(i, (i + 1) % size) for i in range(size - 1)]
        down = [(j, i) for i, j in up]
        last = lax.slice_in_dim(shard, length - width, length, axis=dim)
        initial = lax.slice_in_dim(shard, 0, width, axis=dim)
        before = lax.ppermute(last, axis, up)
        after = lax.ppermute(initial, axis, down)
        shard = jnp.concatenate([before, shard, after], axis=dim)
    return shard


def from_behind(shard, axis, by):
    length = lax.axis_size(axis)
    pairs = [(i, i + by) for i in range(length) if 0 <= i + by < length]
    return lax.ppermute(shard, axis, pairs)


def kernel_values(distance, radius, chirp_rate):
    inside = jnp.abs(distance) <= radius
    phase_arg = chirp_rate / radius * distance * distance
    weight = 1.0 / math.sqrt(2 * radius + 1)
    real_part = jnp.where(inside, jnp.cos(phase_arg) * weight, 0.0)
    imag_part = jnp.where(inside, jnp.sin(phase_arg) * weight, 0.0)
    return (real_part, imag_part)


def row_band(offset, height, margin, conjugate):
    extent = (height, height + 2 * margin)
    target = lax.broadcasted_iota(jnp.int32, extent, 0)
    source = lax.broadcasted_iota(jnp.int32, extent, 1)
    offset_used = -offset if conjugate else offset
    distance = (source - target - margin - offset_used).astype(jnp.float32)
    real_part, imag_part = kernel_values(distance, HALF, CHIRP_ROW)
    return (real_part, -imag_part) if conjugate else (real_part, imag_part)


def column_band(conjugate, block_width):
    extent = (block_width + 2 * HALFCOL, block_width)
    source = lax.broadcasted_iota(jnp.int32, extent, 0)
    target = lax.broadcasted_iota(jnp.int32, extent, 1)
    distance = (source - target - HALFCOL).astype(jnp.float32)
    real_part, imag_part = kernel_values(distance, HALFCOL, CHIRP_COL)
    return (real_part, -imag_part) if conjugate else (real_part, imag_part)


def mix_rows(band, extended):

    def product(matrix, operand):
        return jnp.einsum("ij,mjc->mic", matrix, operand, precision=lax.Precision.HIGHEST)

    real_part = product(band[0], extended[:, 0]) - product(band[1], extended[:, 1])
    imag_part = product(band[0], extended[:, 1]) + product(band[1], extended[:, 0])
    return jnp.stack([real_part, imag_part], axis=1)


def block_product(window, band):

    def product(operand, matrix):
        return jnp.einsum("mrbj,ji->mrbi", operand, matrix, precision=lax.Precision.HIGHEST)

    real_part = product(window[:, 0], band[0]) - product(window[:, 1], band[1])
    imag_part = product(window[:, 1], band[0]) + product(window[:, 0], band[1])
    return jnp.stack([real_part, imag_part], axis=1)


def mix_columns(band, field):
    amount, _, height, columns = field.shape
    blocks = columns // COLBLK
    padded = jnp.pad(field, ((0, 0), (0, 0), (0, 0), (HALFCOL, COLBLK - HALFCOL)))
    middle = padded[..., :columns].reshape(amount, 2, height, blocks, COLBLK)
    beyond = padded[..., COLBLK : columns + COLBLK].reshape(amount, 2, height, blocks, COLBLK)
    window = jnp.concatenate([middle, beyond], axis=4)
    return block_product(window, band).reshape(amount, 2, height, columns)


def rotate(field, cosine, sine):
    real_part = cosine * field[:, 0] - sine * field[:, 1]
    imag_part = cosine * field[:, 1] + sine * field[:, 0]
    return jnp.stack([real_part, imag_part], axis=1)


def slab_forward(field, index_volume, offsets, active):
    margin = HALF + SHIFT
    height = field.shape[2]
    col_band = column_band(False, COLBLK)
    phase_arg = PHASE_SCALE * index_volume[0].astype(jnp.float32)
    transmitted = rotate(field, jnp.cos(phase_arg), jnp.sin(phase_arg))
    stored_fields = [transmitted]
    extended = padded_2(transmitted, (("row", 2),), margin)
    band = row_band(offsets[0], height, margin, False)

    def advance(operand, band=band):
        return mix_columns(col_band, mix_rows(band, operand))

    def remain(operand):
        return operand[:, :, margin : margin + height, :]

    field = lax.cond(active, advance, remain, extended)
    return (field, jnp.stack(stored_fields, axis=0))


def slab_adjoint(adjoint, stored, index_volume, offsets, active):
    margin = HALF + SHIFT
    height = adjoint.shape[2]
    col_band = column_band(True, COLBLK)
    layers = index_volume.shape[0]
    slab_grads = [None] * layers

    def column_step(operand):
        return mix_columns(col_band, operand)

    def unchanged(operand):
        return operand

    def remain(operand):
        return operand[:, :, margin : margin + height, :]

    for layer_no in reversed(range(layers)):
        returned = lax.cond(active, column_step, unchanged, adjoint)
        extended = padded_2(returned, (("row", 2),), margin)
        band = row_band(offsets[layer_no], height, margin, True)

        def row_step(operand, band=band):
            return mix_rows(band, operand)

        returned = lax.cond(active, row_step, remain, extended)
        transmitted = stored[layer_no]
        slab_grads[layer_no] = PHASE_SCALE * jnp.sum(
            transmitted[:, 0] * returned[:, 1] - transmitted[:, 1] * returned[:, 0], axis=0
        )
        phase_arg = PHASE_SCALE * index_volume[layer_no].astype(jnp.float32)
        adjoint = rotate(returned, jnp.cos(phase_arg), -jnp.sin(phase_arg))
    return (adjoint, jnp.stack(slab_grads, axis=0))


def plane_waves(angles, row_start, height, columns, total_rows, total_cols):
    across = angles - TILTS // 2
    along = jnp.mod(3 * angles, TILTS) - TILTS // 2
    row_index = row_start + lax.broadcasted_iota(jnp.int32, (height, columns), 0)
    col_index = lax.broadcasted_iota(jnp.int32, (height, columns), 1)
    period = total_cols * total_rows
    cycles_int = jnp.mod(
        across[:, None, None] * col_index[None] * total_rows
        + along[:, None, None] * row_index[None] * total_cols,
        period,
    )
    phase_arg = 2.0 * math.pi / period * cycles_int.astype(jnp.float32)
    return jnp.stack([jnp.cos(phase_arg), jnp.sin(phase_arg)], axis=1)


def body(index_volume, angles, offsets, measured):
    sections = lax.axis_size("depth")
    section_no = lax.axis_index("depth")
    number = angles.shape[0]
    layers = index_volume.shape[0]
    height = index_volume.shape[1]
    columns = index_volume.shape[2]
    row_start = lax.axis_index("row") * height
    total_rows = height * lax.axis_size("row")
    intensity = measured.astype(jnp.float32)
    grad_init = jnp.zeros((layers, height, columns), jnp.float32)
    incident = plane_waves(angles, row_start, height, columns, total_rows, columns)
    kept_init = jnp.zeros((layers,) + incident.shape, jnp.float32)

    def forward_compute(counter, received, stored, exit_field):
        angle_no = counter - section_no
        active = (angle_no >= 0) & (angle_no < number)
        chosen = jnp.clip(angle_no, 0, number - 1)
        entering = jnp.where(
            section_no == 0, lax.dynamic_slice_in_dim(incident, chosen, 1, 0), received
        )
        result, kept = slab_forward(entering, index_volume, offsets, active)
        placed_kept = lax.dynamic_update_slice_in_dim(stored, kept, chosen, 1)
        stored = jnp.where(active, placed_kept, stored)
        placed = lax.dynamic_update_slice_in_dim(exit_field, result, chosen, 0)
        exit_field = jnp.where(active, placed, exit_field)
        return (result, stored, exit_field)

    def forward_turn(counter, carried):
        result, stored, exit_field = forward_compute(counter, carried[0], carried[1], carried[2])
        return (from_behind(result, "depth", 1), stored, exit_field)

    zero_single = jnp.zeros((1,) + incident.shape[1:], jnp.float32)
    turns = sections + number - 1
    received, stored, exit_field = lax.fori_loop(
        0, turns - 1, forward_turn, (zero_single, kept_init, jnp.zeros_like(incident))
    )
    leftover, stored, exit_field = forward_compute(turns - 1, received, stored, exit_field)
    errors = exit_field[:, 0] * exit_field[:, 0] + exit_field[:, 1] * exit_field[:, 1] - intensity
    exit_adjoint = 2.0 * errors[:, None] * exit_field

    def backward_compute(counter, received, gradient):
        angle_no = counter - (sections - 1 - section_no)
        active = (angle_no >= 0) & (angle_no < number)
        chosen = jnp.clip(angle_no, 0, number - 1)
        entering = jnp.where(
            section_no == sections - 1,
            lax.dynamic_slice_in_dim(exit_adjoint, chosen, 1, 0),
            received,
        )
        result, slab_terms = slab_adjoint(
            entering, lax.dynamic_slice_in_dim(stored, chosen, 1, 1), index_volume, offsets, active
        )
        return (result, jnp.where(active, gradient + slab_terms, gradient))

    def backward_turn(counter, carried):
        result, gradient = backward_compute(counter, carried[0], carried[1])
        return (from_behind(result, "depth", -1), gradient)

    received, gradient = lax.fori_loop(0, turns - 1, backward_turn, (zero_single, grad_init))
    leftover, gradient = backward_compute(turns - 1, received, gradient)
    return gradient


def taps_of(radius, chirp_rate):
    distance = np.arange(-radius, radius + 1, dtype=np.float64)
    phase_arg = chirp_rate / radius * distance * distance
    weight = 1.0 / math.sqrt(2 * radius + 1)
    return (np.cos(phase_arg) * weight, np.sin(phase_arg) * weight)


def column_parts():
    taps = taps_of(HALFCOL, CHIRP_COL)
    source = np.arange(COLBLK + 2 * HALFCOL)[:, None]
    target = np.arange(COLBLK)[None, :]
    place = source - target
    inside = (place >= 0) & (place <= 2 * HALFCOL)
    parts = [np.where(inside, t[np.clip(place, 0, 2 * HALFCOL)], 0.0) for t in taps]
    high = [part.astype(jnp.bfloat16) for part in parts]
    low = [(part - h.astype(np.float64)).astype(jnp.bfloat16) for part, h in zip(parts, high)]
    return [[jnp.asarray(part) for part in pair] for pair in (high, low)]


def column_weights(high, low):
    results = []
    for sign in (1, -1):
        rows = []
        for real_part, imag_part in (high, low):
            rows.append(jnp.concatenate([real_part, sign * imag_part], axis=1))
            rows.append(jnp.concatenate([-sign * imag_part, real_part], axis=1))
        results.append(jnp.concatenate(rows))
    return results


def series(kind, degree):
    nodes = np.cos((np.arange(40) + 0.5) * np.pi / 40) * 8.0 + 8.0
    x = np.sqrt(nodes)
    values = np.cos(PHASE_SCALE * x) if kind == "cos" else np.sin(PHASE_SCALE * x) / x
    fitted = np.polynomial.chebyshev.Chebyshev.fit(nodes, values, degree, domain=[0.0, 16.0])
    return [float(v) for v in fitted.convert(kind=np.polynomial.Polynomial).coef]


COS_SERIES = series("cos", 5)
SIN_SERIES = series("sin", 5)


def evaluate(coefficients, x):
    total = x * coefficients[-1] + coefficients[-2]
    for value in coefficients[-3::-1]:
        total = total * x + value
    return total


def split(x):
    high = x.astype(jnp.bfloat16)
    return (high, (x - high.astype(jnp.float32)).astype(jnp.bfloat16))


def dot(a, b):
    return jnp.dot(a, b, preferred_element_type=jnp.float32)


def row_factor(rows_of, rows_across, offset):
    n = rows_of.shape[0]
    distance = jnp.abs(rows_across - rows_of - offset)
    cosines, sines = taps_of(HALF, CHIRP_ROW)
    real_part = jnp.zeros((n, n), jnp.float32)
    imag_part = jnp.zeros((n, n), jnp.float32)
    for k in range(HALF + 1):
        hit = distance == k
        real_part = jnp.where(hit, float(cosines[HALF + k]), real_part)
        imag_part = jnp.where(hit, float(sines[HALF + k]), imag_part)
    return (real_part, imag_part)


def complex_form(real_part, imag_part):
    upper = jnp.concatenate([real_part, -imag_part], axis=1)
    lower = jnp.concatenate([imag_part, real_part], axis=1)
    return jnp.concatenate([upper, lower], axis=0)


def sweep(sizes, tilts, tiles, own, other, measured, forward_cols, adjoint_cols, mine, theirs, cosine, sine, field, kept):
    slices, planes, height, blocks, broad, columns = sizes
    half = planes * height
    rows = 2 * half
    place = lax.axis_index("depth")
    core = lax.axis_index("row") % 2
    plane = lax.axis_index("row") // 2
    block = plane % 2 * slices + place
    across, along = [jnp.where(core == 0, tilts[i : i + 1, :1], tilts[i : i + 1, 1:]) for i in range(2)]

    def row_numbers(axis):
        i = lax.broadcasted_iota(jnp.int32, (rows, rows), axis)
        side = i // half
        step = (i - side * half) // height
        return 2 * height * (plane ^ step) + height * (core ^ side) + i % height

    rows_of, rows_across = row_numbers(0), row_numbers(1)
    walk_off = [tiles[place ^ s, :1].astype(jnp.int32) for s in range(slices)]
    factors = [[split(part) for part in row_factor(rows_of, rows_across, offset)] for offset in walk_off]
    width = blocks * COLBLK
    cone = 2 * slices * HALFCOL
    first = block * broad - 2 * slices * HALFCOL
    lane = first + lax.broadcasted_iota(jnp.int32, (1, width), 1)
    inside = (lane >= 0) & (lane < columns)

    def wave(count, period):
        count = lax.rem(count, period)
        count = jnp.where(2 * count >= period, count - period, count)
        count = jnp.where(2 * count < -period, count + period, count)
        x = 2.0 * math.pi / period * count.astype(jnp.float32)
        c = evaluate(COS_SERIES, x * x)
        d = evaluate(SIN_SERIES, x * x) * x
        return (1.0 - 2.0 * d * d, 2.0 * c * d)

    row_cos, row_sin = wave(along * rows_of, rows)
    col_cos, col_sin = wave(across * lane, columns)

    def read(level, j):
        return (field[level, j, :, :COLBLK], field[level, j, :, COLBLK:])

    def operand(a, b):
        a_high, a_low = split(a)
        b_high, b_low = split(b)
        return (a_high, b_high, a_low, b_low)

    def mix_cols(level, j, left, right, weights):
        wide = jnp.concatenate([part for pair in zip(left, right) for part in pair], axis=1)
        high, low = wide[:, : 4 * COLBLK], wide[:, 4 * COLBLK :]
        total = dot(high, weights[: 4 * COLBLK]) + (dot(low, weights[: 4 * COLBLK]) + dot(high, weights[4 * COLBLK :]))
        field[level, j] = total

    def mix_rows(factor, blocks_in):
        y = jnp.concatenate([jnp.concatenate([a, b], axis=0) for a, b in blocks_in], axis=1)
        y_high, y_low = split(y)
        v = dot(factor[0], y_high) + (dot(factor[0], y_low) + dot(factor[1], y_high))
        cut = [slice(i * COLBLK, (i + 1) * COLBLK) for i in range(len(blocks_in))]
        middle = v.shape[0] // 2
        return [(v[:middle, c], v[middle:, c]) for c in cut]

    def pairs(n):
        return [range(j, min(j + 2, n)) for j in range(0, n, 2)]

    low_half = lax.broadcasted_iota(jnp.int32, (rows, COLBLK), 1) < HALFCOL

    def forward(s):
        factor = [complex_form(real_part, imag_part) for real_part, imag_part in zip(*factors[s])]
        slot = place ^ s

        def index_block(b):
            cols = slice(b * COLBLK, (b + 1) * COLBLK)
            x = jnp.concatenate([r[slot, :, cols] for r in (own, other)], axis=0).astype(jnp.float32)
            return pltpu.roll(x, HALFCOL, 1) if s % 2 else x

        ahead = index_block(s // 2)
        last = None
        for group in pairs(blocks - s):
            turned = []
            for j in group:
                begin = s * HALFCOL + j * COLBLK
                x = ahead
                if s % 2:
                    ahead = index_block(s // 2 + j + 1)
                    x = jnp.where(low_half, x, ahead)
                elif j + 1 < blocks - s:
                    ahead = index_block(s // 2 + j + 1)
                square = x * x
                c = evaluate(COS_SERIES, square)
                d = evaluate(SIN_SERIES, square) * x
                if begin < cone or begin + COLBLK > cone + broad:
                    seen = inside[:, begin : begin + COLBLK]
                    c, d = jnp.where(seen, c, 0.0), jnp.where(seen, d, 0.0)
                if s > 0:
                    cosine[s, :, j * COLBLK : (j + 1) * COLBLK] = c
                    sine[s, :, j * COLBLK : (j + 1) * COLBLK] = d
                if s == 0:
                    cc, cs = col_cos[:, begin : begin + COLBLK], col_sin[:, begin : begin + COLBLK]
                    a = row_cos * cc - row_sin * cs
                    b = row_cos * cs + row_sin * cc
                else:
                    a, b = read(s - 1, j)
                a, b = c * a - d * b, c * b + d * a
                start = (2 * slices - s) * HALFCOL - j * COLBLK
                later = j - (slices - s)
                if max(start, 0) < min(start + broad, COLBLK):
                    kept[s, later, :rows] = a
                    kept[s, later, rows:] = b
                turned.append((a, b))
            for j, v in zip(group, mix_rows(factor, turned)):
                parts = operand(*v)
                if j > 0:
                    mix_cols(s, j - 1, last, parts, forward_cols)
                last = parts
            yield

    def residual():
        last = None
        for group in pairs(blocks - slices):
            for j in group:
                a, b = read(slices - 1, j)
                cols = slice(j * COLBLK, (j + 1) * COLBLK)
                seen = [measured[k, side, :, cols] for side in range(2) for k in range(planes)]
                seen = jnp.concatenate(seen, axis=0).astype(jnp.float32)
                begin = slices * HALFCOL + j * COLBLK
                error = 2.0 * (a * a + b * b - seen)
                if begin < cone or begin + COLBLK > cone + broad:
                    error = jnp.where(inside[:, begin : begin + COLBLK], error, 0.0)
                parts = operand(error * a, error * b)
                if j > 0:
                    mix_cols(slices, j - 1, last, parts, adjoint_cols)
                last = parts
            yield

    def backward(s):
        factor = [complex_form(real_part.T, -imag_part.T) for real_part, imag_part in zip(*factors[s])]
        if s == 0:
            factor = [
                jnp.concatenate([x[i * half : i * half + 2 * height] for i in range(4)], axis=0) for x in factor
            ]
        level = 2 * slices - 1 - s
        last = None
        for group in pairs(s + broad // COLBLK):
            for j, (a, b) in zip(group, mix_rows(factor, [read(level, j) for j in group])):
                start = s * HALFCOL - j * COLBLK
                lo, hi = max(start, 0), min(start + broad, COLBLK)
                if lo < hi:
                    for i, target in enumerate((mine, theirs)):
                        held = slice(i * half, i * half + 2 * height)
                        there = slice(rows + i * half, rows + i * half + 2 * height)
                        new = slice(i * 2 * height, (i + 1) * 2 * height) if s == 0 else held
                        part = PHASE_SCALE * (kept[s, j, held] * b[new] - kept[s, j, there] * a[new])
                        target[place ^ s, :, lo - start : hi - start] = part[:, lo:hi]
                if s > 0:
                    begin = 2 * (slices - s) * HALFCOL + j * COLBLK
                    c = cosine[s, :, begin : begin + COLBLK]
                    d = sine[s, :, begin : begin + COLBLK]
                    parts = operand(c * a + d * b, c * b - d * a)
                    if j > 0:
                        mix_cols(level + 1, j - 1, last, parts, adjoint_cols)
                    last = parts
            yield

    stages = [forward(s) for s in range(slices)] + [residual()] + [backward(s) for s in reversed(range(slices))]
    counts = [blocks - s for s in range(slices)] + [blocks - slices] + [s + broad // COLBLK for s in reversed(range(slices))]
    order = [(2 * k + t, k) for k, n in enumerate(counts) for t in range(len(pairs(n)))]
    for _, k in sorted(order):
        next(stages[k])


def arrange(sizes, *refs):
    slices, broad = sizes[0], sizes[4]
    place = lax.axis_index("depth")
    group = lax.axis_index("row") // 2 % 2
    out = refs[-1]
    for j in range(slices):
        for i in range(2):
            block = (group ^ i) * slices + (place ^ j)
            out[0, :, pl.ds(pl.multiple_of(block * broad, broad), broad)] = refs[j][i]


def swap(x, axis, step):
    size = lax.axis_size(axis)
    return lax.ppermute(x, axis, [(i, i ^ step) for i in range(size)])


def window_body(index_volume, angles, offsets, measured):
    slices = lax.axis_size("depth")
    planes = lax.axis_size("row") // 2
    place = lax.axis_index("depth")
    core = lax.axis_index("row") % 2
    plane = lax.axis_index("row") // 2
    group = plane % 2
    height, columns = index_volume.shape[1:]
    rows = 2 * planes * height
    half = planes * height
    span = columns // 2
    broad = span // slices
    cone = 2 * slices * HALFCOL
    blocks = (broad + 2 * cone) // COLBLK
    width = blocks * COLBLK

    mine = lax.dynamic_index_in_dim(measured, core, 0, False)
    theirs = swap(lax.dynamic_index_in_dim(measured, 1 - core, 0, False), "row", 1)
    both = jnp.pad(jnp.stack([mine, theirs]), ((0, 0), (0, 0), (cone // 2, cone // 2)))
    first_two = [lax.dynamic_slice_in_dim(both, span * (group ^ i) + broad * place, broad + cone, 2) for i in range(2)]
    weights, first_two = lax.optimization_barrier((column_parts(), first_two))

    far = [
        lax.dynamic_slice_in_dim(index_volume[0], (span - cone) * (group ^ k % 2), span + cone, 1)
        for k in range(planes)
    ]
    far = [
        far[k] if k == 0 else swap(far[k], "row", 2 * k) if k < planes - 1 else swap(index_volume[0], "row", 2 * k)
        for k in range(planes)
    ]
    far[-1] = lax.dynamic_slice_in_dim(far[-1], (span - cone) * group, span + cone, 1)
    tilts = jnp.stack([angles - TILTS // 2, jnp.mod(3 * angles, TILTS) - TILTS // 2])
    weights, tilts, first_two, far = lax.optimization_barrier(
        (column_weights(*weights), tilts, first_two, far)
    )
    far = jnp.pad(jnp.stack(far), ((0, 0), (0, 0), (cone, cone)))
    offset_tile = jnp.broadcast_to(offsets[0].astype(jnp.bfloat16), (planes, height, COLBLK))
    parts = [lax.dynamic_slice_in_dim(far, cone * group + broad * (place ^ j), width, 2) for j in range(slices)]
    own = [jnp.concatenate([part, offset_tile], axis=2) for part in parts]
    last_sent = own[1]
    own = [own[j] if j == 0 else swap(own[j], "depth", j) for j in range(slices)]
    tiles = jnp.stack([x[0, :, width:] for x in own])
    own_first = own[0][:, :, :width].reshape(1, half, width)
    own_later = jnp.stack([x[:, :, :width] for x in own[1:]]).reshape(slices - 1, half, width)
    other_first = swap(own_first, "row", 1)
    other = jnp.concatenate([other_first, swap(own_later, "row", 1)])
    own = jnp.concatenate([own_first, own_later])

    first_two = jnp.stack([first_two[0], swap(first_two[1], "row", 2)])
    first_two, _ = lax.optimization_barrier((first_two, last_sent))
    seen = [first_two] + [swap(first_two, "row", 2 * k) for k in range(2, planes, 2)]
    seen = jnp.concatenate(seen)

    sizes = (slices, planes, height, blocks, broad, columns)
    mine, theirs = pl.pallas_call(
        functools.partial(sweep, sizes),
        out_shape=[jax.ShapeDtypeStruct((slices, 2 * height, broad), jnp.float32)] * 2,
        in_specs=[pl.BlockSpec(memory_space=pltpu.VMEM)] * 7,
        out_specs=[pl.BlockSpec(memory_space=pltpu.VMEM)] * 2,
        scratch_shapes=[
            pltpu.VMEM((slices, rows, width), jnp.float32),
            pltpu.VMEM((slices, rows, width), jnp.float32),
            pltpu.VMEM((2 * slices, blocks - 1, rows, 2 * COLBLK), jnp.float32),
            pltpu.VMEM((slices, slices - 1 + broad // COLBLK, 2 * rows, COLBLK), jnp.float32),
        ],
        compiler_params=pltpu.CompilerParams(vmem_limit_bytes=40 * 1024 * 1024),
    )(tilts, tiles, own, other, seen, *weights)

    summed = mine + swap(theirs, "row", 1)
    parts = jnp.stack([summed[:, :height], swap(summed[:, height:], "row", 2)], axis=1)
    parts = [parts[j] if j == 0 else swap(parts[j], "depth", j) for j in range(slices)]
    return pl.pallas_call(
        functools.partial(arrange, sizes),
        out_shape=jax.ShapeDtypeStruct((1, height, columns), jnp.float32),
        in_specs=[pl.BlockSpec(memory_space=pltpu.VMEM)] * slices,
        out_specs=pl.BlockSpec(memory_space=pltpu.VMEM),
        compiler_params=pltpu.CompilerParams(vmem_limit_bytes=4 * 1024 * 1024),
    )(*parts)


def suits(mesh, index_volume, measured):
    depth, row = mesh.shape["depth"], mesh.shape["row"]
    slices, rows, columns = index_volume.shape
    return (
        slices == depth
        and depth & (depth - 1) == 0
        and row & (row - 1) == 0
        and row > 2
        and measured.shape[0] == 2
        and rows == COLBLK
        and rows // row % 16 == 0
        and columns % (2 * depth * COLBLK) == 0
        and columns >= 4 * depth * HALFCOL
    )


def solution(mesh):
    in_specs = (P("depth", "row", None), P(), P("depth"), P(None, "row", None))
    out_specs = P("depth", "row", None)

    def run(index_volume, angles, offsets, measured):
        chosen = window_body if suits(mesh, index_volume, measured) else body
        mapped = jax.shard_map(chosen, mesh=mesh, in_specs=in_specs, out_specs=out_specs, check_vma=False)
        return mapped(index_volume, angles, offsets, measured)

    return run
```
